512 devices in a mesh: dom: 128 (over y, z, core), sub: 4 (over x).
Axes of the slice: x: 4, y: 8, z: 8, core: 2. Of those that a mesh axis runs over, the one named last changes fastest.
Arguments:
- firm_act: bfloat16 [131072, 512], P('dom', 'sub'), may hold values from -6 to 6
- w_self: bfloat16 [512, 512], replicated, may hold values from -0.25 to 0.25
- w_nbr: bfloat16 [512, 512], replicated, may hold values from -0.25 to 0.25
- halo_rows: int32 [128, 128, 8], P('dom'), may hold values from 0 to 1023
- nbr_index: int32 [131072, 16], P('dom'), may hold values from 0 to 2047
- nbr_count: int32 [131072], P('dom'), may hold values from 1 to 16
- w_pair: bfloat16 [1536, 1024], replicated, may hold values from -0.15625 to 0.15625
- w_out: float32 [1024], replicated, may hold values from -0.9 to 0.9
- push_rows: int32 [128, 128, 4, 2], P('dom'), may hold values from 0 to 1023
- pair_slots: int32 [65536, 2], P(('dom', 'sub')), may hold values from 0 to 255, as said below
- labels: int32 [65536], P(('dom', 'sub')), may hold values 0 or 1
Outputs:
- pair_loss: float32 [65536], P(('dom', 'sub'))
- embed_grad: float32 [131072, 512], P('dom', 'sub')
The draws below stay inside these ranges and needn't reach their ends.
Inputs may be any that keep to these rules, and one draw needn't show every extreme that they name: `halo_rows`: rows of the sending partition's own firms. `nbr_index`: slots of the firm's partition table: its own 1024 rows, then its 1024 halo rows; slots from nbr_count on are unused. `push_rows`: rows of the sending partition's own firms; a firm may be sent several times. `pair_slots`: each pair device's 128 pairs name each of its 256 received slots exactly once.
All inputs are finite; a program needn't handle non-finite values. No bound on the sum of `labels` on one device may be relied on, other than what follows from the above.
Results may differ from the reference program's by a relative error of at most 0.0058.
Values may be sent and summed in bfloat16 or wider, within the bound.
No kernel may reach another device: no remote copies, remote signals or barrier semaphores. Data moves between devices by JAX's collectives and lax.ppermute only.
A program may use at most 64 MiB of HBM per device.

```python
import math
import jax
import jax.numpy as jnp
import numpy as np
from jax import lax

H = 512
DH = 1024
DEG = 16
F_DEV = 1024
HALO_DEV = 1024
PAIR_DEV = 128
SLOT = 8
CAP = 2
N_FIRMS = 131072
PAIRS = 65536
N_DOM = 128
N_SUB = 4


def draw_pair_slots(key, part):
    key = jax.random.fold_in(key, 7)
    device_keys = jax.random.split(key, PAIRS // PAIR_DEV)
    orders = jax.vmap(lambda single: jax.random.permutation(single, 2 * PAIR_DEV))(device_keys)
    return orders.reshape(PAIRS, 2).astype(jnp.int32)


def touch_ends(entries, stream_key, least, high):
    longest = entries.shape.index(max(entries.shape))
    spots = []
    for shift in (0, 1):
        where = [jax.random.randint(jax.random.fold_in(stream_key, axis), (), 0, length) for axis, length in enumerate(entries.shape)]
        where[longest] = (where[longest] + shift) % entries.shape[longest]
        spots.append(tuple(where))
    return entries.at[spots[0]].set(least).at[spots[1]].set(high)


def block_scale(key, shape, cuts, smallest, high):
    def one(axis_at, shards_of):
        draws = jax.random.uniform(jax.random.fold_in(jax.random.fold_in(key, 6), axis_at), (shards_of,), jnp.float32, smallest / len(cuts), high / len(cuts))
        return jnp.repeat(jnp.exp(draws), shape[axis_at] // shards_of).reshape((-1,) + (1,) * (len(shape) - axis_at - 1))

    loudness = one(*cuts[0])
    for cut in cuts[1:]:
        loudness = loudness * one(*cut)
    return loudness


def rank_bounds(amount, lean):
    loads = [(1 << 20) // math.isqrt(grade ** lean) + 1 for grade in range(1, amount + 1)]
    spread = 1 + sum(loads) // (1 << 30)
    return np.cumsum(np.array([max(1, weight // spread) for weight in loads]))


def ranked(key, shape, amount, lean):
    table = rank_bounds(amount, lean)
    ticket = jax.random.randint(jax.random.fold_in(key, 1), shape, 0, int(table[amount - 1]))
    grade = jnp.searchsorted(jnp.asarray(table, jnp.int32), ticket, side="right")
    return jax.random.permutation(jax.random.fold_in(key, 2), amount)[grade].astype(jnp.int32)


def gaussian(own_key, shape, width, most, cuts=(), held_as=jnp.bfloat16):
    loudness = block_scale(own_key, shape, cuts, -0.22, 0.18) if cuts else 1.0
    drawn = jax.random.normal(own_key, shape, jnp.float32) * width * loudness
    return jnp.minimum(jnp.maximum(drawn, -most), most).astype(held_as)


def setup_inputs(seed: int = 0) -> dict:
    key_list = jax.random.split(jax.random.key(seed), 12)
    return {
        "firm_act": gaussian(key_list[0], (N_FIRMS, H), 1.0, 6.0, ((0, 128), (1, 4))),
        "w_self": gaussian(key_list[1], (H, H), H ** -0.5, 0.25),
        "w_nbr": gaussian(key_list[2], (H, H), H ** -0.5, 0.25),
        "halo_rows": touch_ends(jax.random.randint(key_list[3], (N_DOM, N_DOM, SLOT), 0, F_DEV), jax.random.fold_in(key_list[3], 1), 0, F_DEV - 1).astype(jnp.int32),
        "nbr_index": touch_ends(jax.random.randint(key_list[4], (N_FIRMS, DEG), 0, F_DEV + HALO_DEV), jax.random.fold_in(key_list[4], 1), 0, (F_DEV + HALO_DEV) - 1).astype(jnp.int32),
        "nbr_count": touch_ends(jax.random.randint(key_list[5], (N_FIRMS,), 1, DEG + 1), jax.random.fold_in(key_list[5], 1), 1, DEG).astype(jnp.int32),
        "w_pair": gaussian(key_list[6], (3 * H, DH), (3 * H) ** -0.5, 0.15625),
        "w_out": gaussian(key_list[7], (DH,), 0.15, 0.9, (), jnp.float32),
        "push_rows": touch_ends(ranked(key_list[8], (N_DOM, N_DOM, N_SUB, CAP), F_DEV, 2), jax.random.fold_in(key_list[8], 3), 0, F_DEV - 1).astype(jnp.int32),
        "pair_slots": draw_pair_slots(jax.random.fold_in(key_list[11], 71), 0),
        "labels": touch_ends((jax.random.randint(key_list[10], (PAIRS,), 0, 2) < 1).astype(jnp.int32), jax.random.fold_in(key_list[10], 1), 0, 1),
    }


def encode_part(part_index, firm_act, w_self, w_nbr, halo_rows, nbr_index, nbr_count):
    start = (part_index * F_DEV).astype(jnp.int32)
    own_rows = lax.dynamic_slice_in_dim(firm_act, start, F_DEV, 0)
    owners = (jnp.arange(N_DOM, dtype=jnp.int32) * F_DEV)[:, None]
    picks = jnp.take(halo_rows, part_index, axis=1) + owners
    halo = firm_act[picks.reshape(-1)]
    row_table = jnp.concatenate([own_rows, halo], 0)
    index = lax.dynamic_slice_in_dim(nbr_index, start, F_DEV, 0)
    live_count = lax.dynamic_slice_in_dim(nbr_count, start, F_DEV, 0)
    picked = row_table[index].astype(jnp.float32)
    live_mask = (jnp.arange(DEG, dtype=jnp.int32)[None, :] < live_count[:, None]).astype(jnp.float32)
    summed = jnp.einsum("fk,fkc->fc", live_mask, picked, precision=lax.Precision.HIGHEST)
    neighbour = (summed / live_count[:, None].astype(jnp.float32)).astype(jnp.bfloat16)
    embed = jnp.dot(own_rows, w_self, preferred_element_type=jnp.float32) + jnp.dot(neighbour, w_nbr, preferred_element_type=jnp.float32)
    return embed.astype(jnp.bfloat16)


def decode_block(embed, w_pair, w_out, firm_rows, block_labels):
    end_rows = embed[firm_rows].reshape(PAIR_DEV, 2, H)
    left_end = end_rows[:, 0]
    right_end = end_rows[:, 1]
    product = (left_end.astype(jnp.float32) * right_end.astype(jnp.float32)).astype(jnp.bfloat16)
    features = jnp.concatenate([left_end, right_end, product], 1)
    pre_act = jnp.dot(features, w_pair, preferred_element_type=jnp.float32)
    gate_value = jax.nn.sigmoid(pre_act)
    logit = jnp.sum(pre_act * gate_value * w_out[None, :], axis=1)
    target = block_labels.astype(jnp.float32)
    pair_loss = jax.nn.softplus(logit) - target * logit
    outer_grad = jax.nn.sigmoid(logit) - target
    pre_grad = (outer_grad[:, None] * w_out[None, :] * gate_value * (1.0 + pre_act * (1.0 - gate_value))).astype(jnp.bfloat16)
    feat_grad = jnp.dot(pre_grad, w_pair.T, preferred_element_type=jnp.float32)
    left_grad = feat_grad[:, :H] + feat_grad[:, 2 * H:] * right_end.astype(jnp.float32)
    right_grad = feat_grad[:, H:2 * H] + feat_grad[:, 2 * H:] * left_end.astype(jnp.float32)
    end_grads = jnp.stack([left_grad, right_grad], 1).reshape(2 * PAIR_DEV, H).astype(jnp.bfloat16)
    return pair_loss, end_grads


def reference(firm_act, w_self, w_nbr, halo_rows, nbr_index, nbr_count, w_pair, w_out, push_rows, pair_slots, labels):
    embed = lax.map(lambda part_index: encode_part(part_index, firm_act, w_self, w_nbr, halo_rows, nbr_index, nbr_count), jnp.arange(N_DOM, dtype=jnp.int32))
    embed = embed.reshape(N_FIRMS, H)
    device_count = N_DOM * N_SUB
    owner_base = (jnp.arange(N_DOM, dtype=jnp.int32) * F_DEV)[None, None, :, None]
    slot_firms = (owner_base + jnp.transpose(push_rows, (1, 2, 0, 3))).reshape(device_count, 2 * PAIR_DEV)
    slots = pair_slots.reshape(device_count, 2 * PAIR_DEV)
    firms = jnp.take_along_axis(slot_firms, slots, axis=1)
    losses, end_grads = lax.map(lambda pieces: decode_block(embed, w_pair, w_out, pieces[0], pieces[1]), (firms, labels.reshape(device_count, PAIR_DEV)))
    embed_grad = jnp.zeros((N_FIRMS, H), jnp.float32).at[firms.reshape(-1)].add(end_grads.reshape(-1, H).astype(jnp.float32))
    return losses.reshape(PAIRS), embed_grad
```

```python
import jax
import jax.numpy as jnp
from jax import lax
from jax.experimental import pallas as pl
from jax.experimental.pallas import tpu as pltpu
from jax.sharding import PartitionSpec as P

BF = jnp.bfloat16
F32 = jnp.float32
DEAD = 4095
MIB = 1024 * 1024


def contract_first(a, b):
    return lax.dot_general(a, b, (((0,), (0,)), ((), ())), preferred_element_type=F32)


def call(kernel, out_shape, scratch, flops, nbytes, *args):
    return pl.pallas_call(
        kernel,
        out_shape=out_shape,
        scratch_shapes=scratch,
        compiler_params=pltpu.CompilerParams(vmem_limit_bytes=24 * MIB),
        cost_estimate=pl.CostEstimate(flops=flops, bytes_accessed=nbytes, transcendentals=0),
    )(*args)


def halo_kernel(act_ref, rows_ref, out_ref, tmp_ref):
    slots, parts = rows_ref.shape
    rows = rows_ref[...].T
    act = act_ref[...]
    row = lax.broadcasted_iota(jnp.int32, (parts, act.shape[0]), 1)
    for j in range(slots):
        pick = jnp.where(rows[:, j : j + 1] == row, 1.0, 0.0).astype(BF)
        tmp_ref[pl.ds(j, parts, stride=slots), :] = jnp.dot(
            pick, act, preferred_element_type=F32
        )
    out_ref[...] = tmp_ref[...].astype(BF)


def count_kernel(
    act_ref, push_ref, nbr_ref, cnt_ref, near_ref, own_ref, cntp_ref, actp_ref, pick_ref, mine_ref
):
    groups, parts = push_ref.shape
    firms = act_ref.shape[0]
    degree = nbr_ref.shape[0]
    firm = lax.broadcasted_iota(jnp.int32, (firms, parts), 0)
    for b in range(groups):
        pick_ref[:, b * parts : (b + 1) * parts] = jnp.where(
            firm == push_ref[b : b + 1, :], 1.0, 0.0
        ).astype(BF)
    count = cnt_ref[...]
    live = lax.broadcasted_iota(jnp.int32, (degree, firms), 0) < count
    slot = jnp.where(live, nbr_ref[...], DEAD)
    stack = jnp.concatenate(
        [slot >> 4, slot & 15, jnp.broadcast_to(count, (degree, firms))], 0
    ).astype(F32)
    chosen = jnp.dot(stack.astype(BF), pick_ref[...], preferred_element_type=F32)
    wanted = (chosen[:degree] * 16.0 + chosen[degree : 2 * degree]).astype(jnp.int32)
    cntp_ref[...] = chosen[2 * degree : 2 * degree + 8]
    actp_ref[...] = contract_first(act_ref[...], pick_ref[...])
    chunk = 128
    one = jnp.ones((chunk, parts), BF)
    zero = jnp.zeros((chunk, parts), BF)
    base = lax.broadcasted_iota(jnp.int32, (chunk, parts), 0).astype(jnp.int16)
    for b in range(groups):
        lanes = slice(b * parts, (b + 1) * parts)
        want = wanted[:, lanes].astype(jnp.int16)
        spread = [jnp.broadcast_to(want[k : k + 1, :], (chunk, parts)) for k in range(degree)]

        def fill(r, carry, out, first):
            number = base + (first + r * chunk).astype(jnp.int16)
            total = zero
            for k in range(degree):
                total = total + jnp.where(spread[k] == number, one, zero)
            out[pl.ds(pl.multiple_of(r * chunk, chunk), chunk), lanes] = total
            return carry

        lax.fori_loop(0, firms // chunk, lambda r, c: fill(r, c, mine_ref, 0), 0)
        lax.fori_loop(
            0, near_ref.shape[0] // chunk, lambda r, c: fill(r, c, near_ref, firms), 0
        )
    own_ref[...] = contract_first(act_ref[...], mine_ref[...])


def mean_kernel(halo_ref, near_ref, own_ref, cntp_ref, actp_ref, out_ref, tmp_ref):
    groups = 8
    parts = own_ref.shape[1] // groups
    summed = own_ref[...] + contract_first(halo_ref[...], near_ref[...])
    mean = (summed / cntp_ref[0:1, :]).astype(BF).astype(F32)
    for b in range(groups):
        lanes = slice(b * parts, (b + 1) * parts)
        at = (b // 2) * 4 + b % 2
        tmp_ref[pl.ds(at, parts, stride=2 * groups), :] = actp_ref[:, lanes].T
        tmp_ref[pl.ds(at + 2, parts, stride=2 * groups), :] = mean[:, lanes].T
    out_ref[...] = tmp_ref[...].astype(BF)


def decode_kernel(
    recv_ref, self_ref, near_ref, pair_ref, wout_ref, slots_ref, label_ref,
    loss_ref, out_ref, tmp_ref, back_ref,
):
    parts = recv_ref.shape[0] // 16
    pairs = slots_ref.shape[1]
    width = self_ref.shape[0]
    tmp_ref[...] = recv_ref[...].astype(F32)

    def rows_of(kind):
        halves = [
            jnp.concatenate(
                [
                    tmp_ref[pl.ds(s * 4 + kind * 2 + c, parts, stride=16), :]
                    for s in range(4)
                ],
                1,
            )
            for c in range(2)
        ]
        return jnp.concatenate(halves, 0).astype(BF)

    embed = (
        jnp.dot(rows_of(0), self_ref[...], preferred_element_type=F32)
        + jnp.dot(rows_of(1), near_ref[...], preferred_element_type=F32)
    ).astype(BF)
    place = lax.broadcasted_iota(jnp.int32, (2 * parts, pairs), 0)
    slot = jnp.where(place < parts, 2 * place, 2 * (place - parts) + 1)
    left_pick = jnp.where(slot == slots_ref[0:1, :], 1.0, 0.0).astype(BF)
    right_pick = jnp.where(slot == slots_ref[1:2, :], 1.0, 0.0).astype(BF)
    left = contract_first(left_pick, embed)
    right = contract_first(right_pick, embed)
    product = (left * right).astype(BF)
    pre_act = (
        jnp.dot(left.astype(BF), pair_ref[0:width, :], preferred_element_type=F32)
        + jnp.dot(right.astype(BF), pair_ref[width : 2 * width, :], preferred_element_type=F32)
        + jnp.dot(product, pair_ref[2 * width : 3 * width, :], preferred_element_type=F32)
    )
    gate = jax.nn.sigmoid(pre_act)
    wout = wout_ref[...]
    logit = jnp.sum(pre_act * gate * wout, axis=1, keepdims=True)
    target = jnp.broadcast_to(label_ref[...].astype(F32), (pairs, pairs)).T[:, 0:1]
    loss = jnp.maximum(logit, 0.0) + jnp.log1p(jnp.exp(-jnp.abs(logit))) - target * logit
    loss_ref[...] = jnp.broadcast_to(loss, (pairs, pairs)).T[0:1, :]
    outer = jax.nn.sigmoid(logit) - target
    pre_grad = (outer * wout * gate * (1.0 + pre_act * (1.0 - gate))).astype(BF)
    feat = lax.dot_general(
        pre_grad, pair_ref[...], (((1,), (1,)), ((), ())), preferred_element_type=F32
    )
    third = feat[:, 2 * width :]
    left_grad = (feat[:, :width] + third * right).astype(BF)
    right_grad = (feat[:, width : 2 * width] + third * left).astype(BF)
    back = jnp.dot(left_pick, left_grad, preferred_element_type=F32) + jnp.dot(
        right_pick, right_grad, preferred_element_type=F32
    )
    for s in range(4):
        for c in range(2):
            back_ref[pl.ds(s * 2 + c, parts, stride=8), :] = back[
                c * parts : (c + 1) * parts, s * 128 : (s + 1) * 128
            ]
    out_ref[...] = back_ref[...].astype(BF)


def owner_kernel(recv_ref, push_ref, out_ref, tmp_ref):
    groups, parts = push_ref.shape
    tmp_ref[...] = recv_ref[...].astype(F32)
    grads = jnp.concatenate(
        [tmp_ref[pl.ds(b, parts, stride=groups), :] for b in range(groups)], 0
    ).astype(BF)
    firm = lax.broadcasted_iota(jnp.int32, (out_ref.shape[0], parts), 0)
    pick = jnp.concatenate(
        [
            jnp.where(firm == push_ref[b : b + 1, :], 1.0, 0.0).astype(BF)
            for b in range(groups)
        ],
        1,
    )
    out_ref[...] = jnp.dot(pick, grads, preferred_element_type=F32)


def per_device(
    firm_act, w_self, w_nbr, halo_rows, nbr_index, nbr_count, w_pair, w_out, push_rows,
    pair_slots, labels,
):
    firms, narrow = firm_act.shape
    doms, subs, cap = push_rows.shape[1:]
    slots = halo_rows.shape[2]
    both = ("dom", "sub")
    shape = jax.ShapeDtypeStruct
    vmem = pltpu.VMEM
    halo_t = jnp.transpose(halo_rows[0])
    push_t = jnp.transpose(push_rows[0], (1, 2, 0)).reshape(subs * cap, doms)
    pushed = doms * subs * cap
    halos = doms * slots

    outgoing = call(
        halo_kernel, shape((halos, narrow), BF), [vmem((halos, narrow), F32)],
        2 * halos * firms * narrow, 600_000, firm_act, halo_t,
    )
    incoming = lax.all_to_all(
        outgoing.reshape(doms, slots, narrow), "dom", 0, 0, tiled=True
    ).reshape(halos, narrow)
    near_counts, own_sum, push_count, push_act = call(
        count_kernel,
        (
            shape((halos, pushed), BF), shape((narrow, pushed), F32),
            shape((8, pushed), F32), shape((narrow, pushed), F32),
        ),
        [vmem((firms, pushed), BF), vmem((firms, pushed), BF)],
        10_000_000_000, 4_000_000,
        firm_act, push_t, jnp.transpose(nbr_index), nbr_count.reshape(1, firms),
    )
    message = call(
        mean_kernel, shape((2 * pushed, narrow), BF), [vmem((2 * pushed, narrow), F32)],
        2 * halos * pushed * narrow, 4_000_000,
        incoming, near_counts, own_sum, push_count, push_act,
    )
    arrived = lax.all_to_all(
        message.reshape(doms * subs, 2 * cap, narrow), both, 0, 0, tiled=True
    ).reshape(2 * pushed, narrow)
    pairs = labels.shape[0]
    pair_loss, back = call(
        decode_kernel,
        (shape((1, pairs), F32), shape((pushed, narrow), BF)),
        [vmem((2 * pushed, narrow), F32), vmem((pushed, narrow), F32)],
        1_200_000_000, 5_000_000,
        arrived, w_self, w_nbr, w_pair, w_out.reshape(1, -1), jnp.transpose(pair_slots),
        labels.reshape(1, pairs),
    )
    returned = lax.all_to_all(
        back.reshape(doms * subs, cap, narrow), both, 0, 0, tiled=True
    ).reshape(pushed, narrow)
    embed_grad = call(
        owner_kernel, shape((firms, narrow), F32), [vmem((pushed, narrow), F32)],
        2 * pushed * firms * narrow, 1_000_000, returned, push_t,
    )
    return (pair_loss.reshape(pairs), embed_grad)


def solution(mesh):
    in_specs = (
        P("dom", "sub"), P(), P(), P("dom", None, None), P("dom", None), P("dom"), P(), P(),
        P("dom", None, None, None), P(("dom", "sub"), None), P(("dom", "sub")),
    )
    out_specs = (P(("dom", "sub")), P("dom", "sub"))
    return jax.shard_map(
        per_device, mesh=mesh, in_specs=in_specs, out_specs=out_specs, check_vma=False
    )
```

```python
import jax
import jax.numpy as jnp
from jax import lax
from jax.experimental import pallas as pl
from jax.experimental.pallas import tpu as pltpu
from jax.sharding import PartitionSpec as P

BF = jnp.bfloat16
F32 = jnp.float32
DEAD = 4095
MIB = 1024 * 1024


def contract_first(a, b):
    return lax.dot_general(a, b, (((0,), (0,)), ((), ())), preferred_element_type=F32)


def call(kernel, out_shape, scratch, flops, nbytes, *args, in_specs=None, out_specs=None):
    where = {"hbm": pl.ANY, "vmem": pltpu.VMEM}
    specs = {}
    if in_specs is not None:
        args = [
            pltpu.with_memory_space_constraint(a, pltpu.HBM) if w[0] == "hbm" else a
            for a, w in zip(args, in_specs)
        ]
        specs["in_specs"] = [pl.BlockSpec(memory_space=where[w[-1]]) for w in in_specs]
    if out_specs is not None:
        specs["out_specs"] = [pl.BlockSpec(memory_space=where[w]) for w in out_specs]
    return pl.pallas_call(
        kernel,
        out_shape=out_shape,
        scratch_shapes=scratch,
        **specs,
        compiler_params=pltpu.CompilerParams(vmem_limit_bytes=24 * MIB),
        cost_estimate=pl.CostEstimate(flops=flops, bytes_accessed=nbytes, transcendentals=0),
    )(*args)


def halo_kernel(act_ref, rows_ref, out_ref, tmp_ref):
    slots, parts = rows_ref.shape
    rows = rows_ref[...].T
    act = act_ref[...]
    row = lax.broadcasted_iota(jnp.int32, (parts, act.shape[0]), 1)
    for j in range(slots):
        pick = jnp.where(rows[:, j : j + 1] == row, 1.0, 0.0).astype(BF)
        tmp_ref[pl.ds(j, parts, stride=slots), :] = jnp.dot(
            pick, act, preferred_element_type=F32
        )
    out_ref[...] = tmp_ref[...].astype(BF)


def count_kernel(
    act_ref, push_ref, nbr_ref, cnt_ref, near_out, own_out, actp_out, cntp_ref,
    near_ref, own_ref, actp_ref, pick_ref, mine_ref, sems,
):
    groups, parts = push_ref.shape
    firms = act_ref.shape[0]
    degree = nbr_ref.shape[0]
    firm = lax.broadcasted_iota(jnp.int32, (firms, parts), 0)
    for b in range(groups):
        pick_ref[:, b * parts : (b + 1) * parts] = jnp.where(
            firm == push_ref[b : b + 1, :], 1.0, 0.0
        ).astype(BF)
    count = cnt_ref[...]
    live = lax.broadcasted_iota(jnp.int32, (degree, firms), 0) < count
    slot = jnp.where(live, nbr_ref[...], DEAD)
    stack = jnp.concatenate(
        [slot >> 4, slot & 15, jnp.broadcast_to(count, (degree, firms))], 0
    ).astype(F32)
    chosen = jnp.dot(stack.astype(BF), pick_ref[...], preferred_element_type=F32)
    wanted = (chosen[:degree] * 16.0 + chosen[degree : 2 * degree]).astype(jnp.int32)
    cntp_ref[...] = chosen[2 * degree : 2 * degree + 8]
    actp_ref[...] = contract_first(act_ref[...], pick_ref[...])
    copies = [pltpu.make_async_copy(actp_ref, actp_out, sems.at[groups])]
    copies[0].start()
    chunk = 128
    one = jnp.ones((chunk, parts), BF)
    zero = jnp.zeros((chunk, parts), BF)
    base = lax.broadcasted_iota(jnp.int32, (chunk, parts), 0).astype(jnp.int16)
    for b in range(groups):
        lanes = slice(b * parts, (b + 1) * parts)
        want = wanted[:, lanes].astype(jnp.int16)
        spread = [jnp.broadcast_to(want[k : k + 1, :], (chunk, parts)) for k in range(degree)]

        def fill(r, carry, out, first):
            number = base + (first + r * chunk).astype(jnp.int16)
            total = zero
            for k in range(degree):
                total = total + jnp.where(spread[k] == number, one, zero)
            out[pl.ds(pl.multiple_of(r * chunk, chunk), chunk), lanes] = total
            return carry

        lax.fori_loop(0, firms // chunk, lambda r, c: fill(r, c, mine_ref, 0), 0)
        lax.fori_loop(
            0, near_ref.shape[0] // chunk, lambda r, c: fill(r, c, near_ref, firms), 0
        )
        copies.append(
            pltpu.make_async_copy(near_ref.at[:, lanes], near_out.at[:, lanes], sems.at[b])
        )
        copies[-1].start()
    own_ref[...] = contract_first(act_ref[...], mine_ref[...])
    copies.append(pltpu.make_async_copy(own_ref, own_out, sems.at[groups + 1]))
    copies[-1].start()
    for copy in copies:
        copy.wait()


def mean_kernel(
    halo_ref, near_in, own_in, actp_in, cntp_ref, out_ref, tmp_ref, near_ref, own_ref, actp_ref, sems
):
    groups = 8
    parts = own_ref.shape[1] // groups
    parcels = 4
    step = near_ref.shape[0] // parcels
    act_copy = pltpu.make_async_copy(actp_in, actp_ref, sems.at[parcels])
    own_copy = pltpu.make_async_copy(own_in, own_ref, sems.at[parcels + 1])
    copies = [
        pltpu.make_async_copy(
            near_in.at[pl.ds(i * step, step), :], near_ref.at[pl.ds(i * step, step), :], sems.at[i]
        )
        for i in range(parcels)
    ]
    act_copy.start()
    own_copy.start()
    for copy in copies:
        copy.start()
    act_copy.wait()
    for b in range(groups):
        lanes = slice(b * parts, (b + 1) * parts)
        at = (b // 2) * 4 + b % 2
        tmp_ref[pl.ds(at, parts, stride=2 * groups), :] = actp_ref[:, lanes].T
    own_copy.wait()
    summed = own_ref[...]
    for i, copy in enumerate(copies):
        copy.wait()
        rows = slice(i * step, (i + 1) * step)
        summed = summed + contract_first(halo_ref[rows, :], near_ref[rows, :])
    mean = (summed / cntp_ref[0:1, :]).astype(BF).astype(F32)
    for b in range(groups):
        lanes = slice(b * parts, (b + 1) * parts)
        at = (b // 2) * 4 + b % 2 + 2
        tmp_ref[pl.ds(at, parts, stride=2 * groups), :] = mean[:, lanes].T
    out_ref[...] = tmp_ref[...].astype(BF)


def decode_kernel(
    recv_ref, self_ref, near_ref, pair_ref, wout_ref, slots_ref, label_ref,
    loss_ref, out_ref, tmp_ref, back_ref,
):
    parts = recv_ref.shape[0] // 16
    pairs = slots_ref.shape[1]
    width = self_ref.shape[0]
    tmp_ref[...] = recv_ref[...].astype(F32)

    def rows_of(kind):
        halves = [
            jnp.concatenate(
                [
                    tmp_ref[pl.ds(s * 4 + kind * 2 + c, parts, stride=16), :]
                    for s in range(4)
                ],
                1,
            )
            for c in range(2)
        ]
        return jnp.concatenate(halves, 0).astype(BF)

    embed = (
        jnp.dot(rows_of(0), self_ref[...], preferred_element_type=F32)
        + jnp.dot(rows_of(1), near_ref[...], preferred_element_type=F32)
    ).astype(BF)
    place = lax.broadcasted_iota(jnp.int32, (2 * parts, pairs), 0)
    slot = jnp.where(place < parts, 2 * place, 2 * (place - parts) + 1)
    left_pick = jnp.where(slot == slots_ref[0:1, :], 1.0, 0.0).astype(BF)
    right_pick = jnp.where(slot == slots_ref[1:2, :], 1.0, 0.0).astype(BF)
    left = contract_first(left_pick, embed)
    right = contract_first(right_pick, embed)
    product = (left * right).astype(BF)
    pre_act = (
        jnp.dot(left.astype(BF), pair_ref[0:width, :], preferred_element_type=F32)
        + jnp.dot(right.astype(BF), pair_ref[width : 2 * width, :], preferred_element_type=F32)
        + jnp.dot(product, pair_ref[2 * width : 3 * width, :], preferred_element_type=F32)
    )
    gate = jax.nn.sigmoid(pre_act)
    wout = wout_ref[...]
    logit = jnp.sum(pre_act * gate * wout, axis=1, keepdims=True)
    target = jnp.broadcast_to(label_ref[...].astype(F32), (pairs, pairs)).T[:, 0:1]
    loss = jnp.maximum(logit, 0.0) + jnp.log1p(jnp.exp(-jnp.abs(logit))) - target * logit
    loss_ref[...] = jnp.broadcast_to(loss, (pairs, pairs)).T[0:1, :]
    outer = jax.nn.sigmoid(logit) - target
    pre_grad = (outer * wout * gate * (1.0 + pre_act * (1.0 - gate))).astype(BF)
    feat = lax.dot_general(
        pre_grad, pair_ref[...], (((1,), (1,)), ((), ())), preferred_element_type=F32
    )
    third = feat[:, 2 * width :]
    left_grad = (feat[:, :width] + third * right).astype(BF)
    right_grad = (feat[:, width : 2 * width] + third * left).astype(BF)
    back = jnp.dot(left_pick, left_grad, preferred_element_type=F32) + jnp.dot(
        right_pick, right_grad, preferred_element_type=F32
    )
    for s in range(4):
        for c in range(2):
            back_ref[pl.ds(s * 2 + c, parts, stride=8), :] = back[
                c * parts : (c + 1) * parts, s * 128 : (s + 1) * 128
            ]
    out_ref[...] = back_ref[...].astype(BF)


def owner_kernel(recv_ref, push_ref, out_ref, tmp_ref):
    groups, parts = push_ref.shape
    tmp_ref[...] = recv_ref[...].astype(F32)
    grads = jnp.concatenate(
        [tmp_ref[pl.ds(b, parts, stride=groups), :] for b in range(groups)], 0
    ).astype(BF)
    firm = lax.broadcasted_iota(jnp.int32, (out_ref.shape[0], parts), 0)
    pick = jnp.concatenate(
        [
            jnp.where(firm == push_ref[b : b + 1, :], 1.0, 0.0).astype(BF)
            for b in range(groups)
        ],
        1,
    )
    out_ref[...] = jnp.dot(pick, grads, preferred_element_type=F32)


def per_device(
    firm_act, w_self, w_nbr, halo_rows, nbr_index, nbr_count, w_pair, w_out, push_rows,
    pair_slots, labels,
):
    firms, narrow = firm_act.shape
    doms, subs, cap = push_rows.shape[1:]
    slots = halo_rows.shape[2]
    both = ("dom", "sub")
    shape = jax.ShapeDtypeStruct
    vmem = pltpu.VMEM
    halo_t = jnp.transpose(halo_rows[0])
    push_t = jnp.transpose(push_rows[0], (1, 2, 0)).reshape(subs * cap, doms)
    pushed = doms * subs * cap
    halos = doms * slots

    hbm = pltpu.HBM
    sems = pltpu.SemaphoreType.DMA
    fetch = ("hbm", "vmem")
    outgoing = call(
        halo_kernel, shape((halos, narrow), BF), [vmem((halos, narrow), F32)],
        2 * halos * firms * narrow, 600_000, firm_act, halo_t, in_specs=[fetch, fetch],
    )
    incoming = lax.all_to_all(
        outgoing.reshape(doms, slots, narrow), "dom", 0, 0, tiled=True
    ).reshape(halos, narrow)
    near_counts, own_sum, push_act, push_count = call(
        count_kernel,
        (
            hbm((halos, pushed), BF), hbm((narrow, pushed), F32), hbm((narrow, pushed), F32),
            shape((8, pushed), F32),
        ),
        [
            vmem((halos, pushed), BF), vmem((narrow, pushed), F32), vmem((narrow, pushed), F32),
            vmem((firms, pushed), BF), vmem((firms, pushed), BF), sems((subs * cap + 2,)),
        ],
        10_000_000_000, 4_000_000,
        firm_act, push_t, jnp.transpose(nbr_index), nbr_count.reshape(1, firms),
        in_specs=[fetch] * 4, out_specs=["hbm"] * 3 + ["vmem"],
    )
    message = call(
        mean_kernel, shape((2 * pushed, narrow), BF),
        [
            vmem((2 * pushed, narrow), F32), vmem((halos, pushed), BF), vmem((narrow, pushed), F32),
            vmem((narrow, pushed), F32), sems((6,)),
        ],
        2 * halos * pushed * narrow, 4_000_000,
        incoming, near_counts, own_sum, push_act, push_count,
        in_specs=[("vmem",)] + [("hbm",)] * 3 + [("vmem",)],
    )
    arrived = lax.all_to_all(
        message.reshape(doms * subs, 2 * cap, narrow), both, 0, 0, tiled=True
    ).reshape(2 * pushed, narrow)
    pairs = labels.shape[0]
    pair_loss, back = call(
        decode_kernel,
        (shape((1, pairs), F32), shape((pushed, narrow), BF)),
        [vmem((2 * pushed, narrow), F32), vmem((pushed, narrow), F32)],
        1_200_000_000, 5_000_000,
        arrived, w_self, w_nbr, w_pair, w_out.reshape(1, -1), jnp.transpose(pair_slots),
        labels.reshape(1, pairs),
    )
    returned = lax.all_to_all(
        back.reshape(doms * subs, cap, narrow), both, 0, 0, tiled=True
    ).reshape(pushed, narrow)
    embed_grad = call(
        owner_kernel, shape((firms, narrow), F32), [vmem((pushed, narrow), F32)],
        2 * pushed * firms * narrow, 1_000_000, returned, push_t,
    )
    return (pair_loss.reshape(pairs), embed_grad)


def solution(mesh):
    in_specs = (
        P("dom", "sub"), P(), P(), P("dom", None, None), P("dom", None), P("dom"), P(), P(),
        P("dom", None, None, None), P(("dom", "sub"), None), P(("dom", "sub")),
    )
    out_specs = (P(("dom", "sub")), P("dom", "sub"))
    return jax.shard_map(
        per_device, mesh=mesh, in_specs=in_specs, out_specs=out_specs, check_vma=False
    )
```

```python
import jax
import jax.numpy as jnp
from jax import lax
from jax.experimental import pallas as pl
from jax.experimental.pallas import tpu as pltpu
from jax.sharding import PartitionSpec as P

BF = jnp.bfloat16
F32 = jnp.float32
DEAD = 4095
MIB = 1024 * 1024


def contract_first(a, b):
    return lax.dot_general(a, b, (((0,), (0,)), ((), ())), preferred_element_type=F32)


def call(kernel, out_shape, scratch, flops, nbytes, *args, in_specs=None, out_specs=None):
    where = {"hbm": pl.ANY, "vmem": pltpu.VMEM}
    specs = {}
    if in_specs is not None:
        args = [
            pltpu.with_memory_space_constraint(a, pltpu.HBM) if w[0] == "hbm" else a
            for a, w in zip(args, in_specs)
        ]
        specs["in_specs"] = [pl.BlockSpec(memory_space=where[w[-1]]) for w in in_specs]
    if out_specs is not None:
        specs["out_specs"] = [pl.BlockSpec(memory_space=where[w]) for w in out_specs]
    return pl.pallas_call(
        kernel,
        out_shape=out_shape,
        scratch_shapes=scratch,
        **specs,
        compiler_params=pltpu.CompilerParams(vmem_limit_bytes=24 * MIB),
        cost_estimate=pl.CostEstimate(flops=flops, bytes_accessed=nbytes, transcendentals=0),
    )(*args)


def one_hot_rows(columns, width):
    number = lax.broadcasted_iota(jnp.int32, (columns.shape[0], width), 1)
    return [
        jnp.where(columns[:, j : j + 1] == number, 1.0, 0.0).astype(BF)
        for j in range(columns.shape[1])
    ]


def halo_kernel(act_ref, rows_ref, out_ref, tmp_ref, pick_ref):
    slots, parts = rows_ref.shape
    for j, rows in enumerate(one_hot_rows(rows_ref[...].T, act_ref.shape[0])):
        pick_ref[j * parts : (j + 1) * parts, :] = rows
    picked = jnp.dot(pick_ref[...], act_ref[...], preferred_element_type=F32)
    for j in range(slots):
        tmp_ref[pl.ds(j, parts, stride=slots), :] = picked[j * parts : (j + 1) * parts]
    out_ref[...] = tmp_ref[...].astype(BF)


def count_kernel(
    act_ref, push_ref, nbr_ref, cnt_ref, near_out, own_out, actp_out, cntp_ref,
    near_ref, own_ref, actp_ref, pick_ref, mine_ref, where_ref, sems,
):
    groups, parts = push_ref.shape
    firms = act_ref.shape[0]
    degree = nbr_ref.shape[0]
    pushed = groups * parts
    i32, i16 = jnp.int32, jnp.int16
    for j, rows in enumerate(one_hot_rows(push_ref[...].T, firms)):
        pick_ref[j * parts : (j + 1) * parts, :] = rows
    pick = pick_ref[...]
    count = cnt_ref[...]
    live = lax.broadcasted_iota(i32, (degree, firms), 0) < count
    slot = jnp.where(live, nbr_ref[...], DEAD)
    counts = jnp.broadcast_to(count, (degree, firms))
    stack = jnp.concatenate([slot >> 7, slot & 127, counts], 0).astype(F32).astype(BF)
    chosen = lax.dot_general(
        pick, stack, (((1,), (1,)), ((), ())), preferred_element_type=F32
    )
    for j in range(groups):
        block = chosen[j * parts : (j + 1) * parts, 2 * degree : 3 * degree]
        cntp_ref[j : j + 1, :] = block.T[0:1, :]
    actp_ref[...] = jnp.dot(pick, act_ref[...], preferred_element_type=F32).astype(BF)
    copies = [pltpu.make_async_copy(actp_ref, actp_out, sems.at[0])]
    copies[0].start()
    batch = 16
    span = batch * degree
    shape = (2 * degree, 2 * span)
    lane = lax.broadcasted_iota(i32, shape, 1)
    spread = jnp.where(
        lax.broadcasted_iota(i32, shape, 0) == (lane // span) * degree + lane % degree, 1.0, 0.0
    ).astype(BF)
    wide = jnp.dot(chosen[:, : 2 * degree].astype(BF), spread, preferred_element_type=F32)
    row = lax.broadcasted_iota(i32, (pushed, 2 * span), 0) % batch
    lane = (lax.broadcasted_iota(i32, (pushed, 2 * span), 1) % span) // degree
    wide = jnp.where(row == lane, wide, 0.0).astype(BF)
    shape = (pushed // batch, pushed)
    gather = jnp.where(
        lax.broadcasted_iota(i32, shape, 1) // batch == lax.broadcasted_iota(i32, shape, 0), 1.0, 0.0
    ).astype(BF)
    where_ref[...] = jnp.dot(gather, wide, preferred_element_type=F32)
    own_row = (
        lax.broadcasted_iota(i32, (batch, span), 1) // degree
        == lax.broadcasted_iota(i32, (batch, span), 0)
    )
    low_number = lax.broadcasted_iota(i32, (128, span), 0).astype(i16)
    one = jnp.ones((batch, span), BF)
    zero = jnp.zeros((batch, span), BF)
    mine_blocks = firms // 128
    near_blocks = near_ref.shape[1] // 128

    def fill(g, carry):
        line = where_ref[pl.ds(g, 1), :]
        high = jnp.where(own_row, jnp.broadcast_to(line[:, :span], (batch, span)), -1.0)
        high = high.astype(i32).astype(i16)
        lhs = jnp.concatenate(
            [jnp.where(high == i16(h), one, zero) for h in range(mine_blocks + near_blocks)], 0
        )
        low = jnp.broadcast_to(line[:, span:], (128, span)).astype(i32).astype(i16)
        rhs = jnp.where(low == low_number, jnp.ones((128, span), BF), jnp.zeros((128, span), BF))
        counts = lax.dot_general(
            lhs, rhs, (((1,), (1,)), ((), ())), preferred_element_type=F32
        ).astype(BF)
        rows = pl.ds(pl.multiple_of(g * batch, batch), batch)
        for h in range(mine_blocks):
            mine_ref[rows, h * 128 : (h + 1) * 128] = counts[h * batch : (h + 1) * batch]
        for h in range(near_blocks):
            at = (mine_blocks + h) * batch
            near_ref[rows, h * 128 : (h + 1) * 128] = counts[at : at + batch]
        return carry

    parcels = 4
    each = pushed // batch // parcels
    for p in range(parcels):
        lax.fori_loop(p * each, (p + 1) * each, fill, 0, unroll=4)
        rows = pl.ds(p * each * batch, each * batch)
        copies.append(pltpu.make_async_copy(near_ref.at[rows, :], near_out.at[rows, :], sems.at[1 + p]))
        copies[-1].start()
    own_ref[...] = jnp.dot(mine_ref[...], act_ref[...], preferred_element_type=F32)
    copies.append(pltpu.make_async_copy(own_ref, own_out, sems.at[1 + parcels]))
    copies[-1].start()
    for copy in copies:
        copy.wait()


def mean_kernel(
    halo_ref, near_in, own_in, actp_in, cntp_ref, out_ref, tmp_ref, near_ref, own_ref, actp_ref, sems
):
    groups, parts = cntp_ref.shape
    parcels = 4
    step = near_ref.shape[0] // parcels
    act_copy = pltpu.make_async_copy(actp_in, actp_ref, sems.at[parcels])
    own_copy = pltpu.make_async_copy(own_in, own_ref, sems.at[parcels + 1])
    copies = [
        pltpu.make_async_copy(
            near_in.at[pl.ds(i * step, step), :], near_ref.at[pl.ds(i * step, step), :], sems.at[i]
        )
        for i in range(parcels)
    ]
    act_copy.start()
    own_copy.start()
    for copy in copies:
        copy.start()
    divisor = cntp_ref[...].T
    halo = halo_ref[...]

    def place(b, rows, kind):
        tmp_ref[pl.ds((b // 2) * 4 + kind * 2 + b % 2, parts, stride=2 * groups), :] = rows

    act_copy.wait()
    for b in range(groups):
        place(b, actp_ref[b * parts : (b + 1) * parts, :].astype(F32), 0)
    own_copy.wait()
    for i, copy in enumerate(copies):
        copy.wait()
        rows = slice(i * step, (i + 1) * step)
        summed = own_ref[rows, :] + jnp.dot(near_ref[rows, :], halo, preferred_element_type=F32)
        for j in range(step // parts):
            b = i * (step // parts) + j
            mean = summed[j * parts : (j + 1) * parts] / divisor[:, b : b + 1]
            place(b, mean.astype(BF).astype(F32), 1)
    out_ref[...] = tmp_ref[...].astype(BF)


def decode_kernel(
    recv_ref, self_ref, near_ref, pair_ref, wout_ref, slots_ref, label_ref,
    loss_ref, out_ref, tmp_ref, back_ref,
):
    parts = recv_ref.shape[0] // 16
    pairs = slots_ref.shape[1]
    width = self_ref.shape[0]
    tmp_ref[...] = recv_ref[...].astype(F32)

    def rows_of(kind):
        halves = [
            jnp.concatenate(
                [
                    tmp_ref[pl.ds(s * 4 + kind * 2 + c, parts, stride=16), :]
                    for s in range(4)
                ],
                1,
            )
            for c in range(2)
        ]
        return jnp.concatenate(halves, 0).astype(BF)

    embed = (
        jnp.dot(rows_of(0), self_ref[...], preferred_element_type=F32)
        + jnp.dot(rows_of(1), near_ref[...], preferred_element_type=F32)
    ).astype(BF)
    place = lax.broadcasted_iota(jnp.int32, (2 * parts, pairs), 0)
    slot = jnp.where(place < parts, 2 * place, 2 * (place - parts) + 1)
    left_pick = jnp.where(slot == slots_ref[0:1, :], 1.0, 0.0).astype(BF)
    right_pick = jnp.where(slot == slots_ref[1:2, :], 1.0, 0.0).astype(BF)
    left = contract_first(left_pick, embed)
    right = contract_first(right_pick, embed)
    product = (left * right).astype(BF)
    pre_act = (
        jnp.dot(left.astype(BF), pair_ref[0:width, :], preferred_element_type=F32)
        + jnp.dot(right.astype(BF), pair_ref[width : 2 * width, :], preferred_element_type=F32)
        + jnp.dot(product, pair_ref[2 * width : 3 * width, :], preferred_element_type=F32)
    )
    gate = jax.nn.sigmoid(pre_act)
    wout = wout_ref[...]
    logit = jnp.sum(pre_act * gate * wout, axis=1, keepdims=True)
    target = jnp.broadcast_to(label_ref[...].astype(F32), (pairs, pairs)).T[:, 0:1]
    loss = jnp.maximum(logit, 0.0) + jnp.log1p(jnp.exp(-jnp.abs(logit))) - target * logit
    loss_ref[...] = jnp.broadcast_to(loss, (pairs, pairs)).T[0:1, :]
    outer = jax.nn.sigmoid(logit) - target
    pre_grad = (outer * wout * gate * (1.0 + pre_act * (1.0 - gate))).astype(BF)
    feat = lax.dot_general(
        pre_grad, pair_ref[...], (((1,), (1,)), ((), ())), preferred_element_type=F32
    )
    third = feat[:, 2 * width :]
    left_grad = (feat[:, :width] + third * right).astype(BF)
    right_grad = (feat[:, width : 2 * width] + third * left).astype(BF)
    back = jnp.dot(left_pick, left_grad, preferred_element_type=F32) + jnp.dot(
        right_pick, right_grad, preferred_element_type=F32
    )
    for s in range(4):
        for c in range(2):
            back_ref[pl.ds(s * 2 + c, parts, stride=8), :] = back[
                c * parts : (c + 1) * parts, s * 128 : (s + 1) * 128
            ]
    out_ref[...] = back_ref[...].astype(BF)


def owner_kernel(recv_ref, push_ref, out_ref, tmp_ref):
    groups, parts = push_ref.shape
    tmp_ref[...] = recv_ref[...].astype(F32)
    grads = jnp.concatenate(
        [tmp_ref[pl.ds(b, parts, stride=groups), :] for b in range(groups)], 0
    ).astype(BF)
    firm = lax.broadcasted_iota(jnp.int32, (out_ref.shape[0], parts), 0)
    pick = jnp.concatenate(
        [
            jnp.where(firm == push_ref[b : b + 1, :], 1.0, 0.0).astype(BF)
            for b in range(groups)
        ],
        1,
    )
    out_ref[...] = jnp.dot(pick, grads, preferred_element_type=F32)


def per_device(
    firm_act, w_self, w_nbr, halo_rows, nbr_index, nbr_count, w_pair, w_out, push_rows,
    pair_slots, labels,
):
    firms, narrow = firm_act.shape
    doms, subs, cap = push_rows.shape[1:]
    slots = halo_rows.shape[2]
    both = ("dom", "sub")
    shape = jax.ShapeDtypeStruct
    vmem = pltpu.VMEM
    halo_t = jnp.transpose(halo_rows[0])
    push_t = jnp.transpose(push_rows[0], (1, 2, 0)).reshape(subs * cap, doms)
    pushed = doms * subs * cap
    halos = doms * slots

    hbm = pltpu.HBM
    sems = pltpu.SemaphoreType.DMA
    fetch = ("hbm", "vmem")
    outgoing = call(
        halo_kernel, shape((halos, narrow), BF),
        [vmem((halos, narrow), F32), vmem((halos, firms), BF)],
        2 * halos * firms * narrow, 600_000, firm_act, halo_t, in_specs=[fetch, fetch],
    )
    incoming = lax.all_to_all(
        outgoing.reshape(doms, slots, narrow), "dom", 0, 0, tiled=True
    ).reshape(halos, narrow)
    near_counts, own_sum, push_act, push_count = call(
        count_kernel,
        (
            hbm((pushed, halos), BF), hbm((pushed, narrow), F32), hbm((pushed, narrow), BF),
            shape((subs * cap, doms), F32),
        ),
        [
            vmem((pushed, halos), BF), vmem((pushed, narrow), F32), vmem((pushed, narrow), BF),
            vmem((pushed, firms), BF), vmem((pushed, firms), BF), vmem((pushed // 16, 512), F32),
            sems((6,)),
        ],
        10_000_000_000, 4_000_000,
        firm_act, push_t, jnp.transpose(nbr_index), nbr_count.reshape(1, firms),
        in_specs=[fetch] * 4, out_specs=["hbm"] * 3 + ["vmem"],
    )
    message = call(
        mean_kernel, shape((2 * pushed, narrow), BF),
        [
            vmem((2 * pushed, narrow), F32), vmem((pushed, halos), BF), vmem((pushed, narrow), F32),
            vmem((pushed, narrow), BF), sems((6,)),
        ],
        2 * halos * pushed * narrow, 4_000_000,
        incoming, near_counts, own_sum, push_act, push_count,
        in_specs=[("vmem",)] + [("hbm",)] * 3 + [("vmem",)],
    )
    arrived = lax.all_to_all(
        message.reshape(doms * subs, 2 * cap, narrow), both, 0, 0, tiled=True
    ).reshape(2 * pushed, narrow)
    pairs = labels.shape[0]
    pair_loss, back = call(
        decode_kernel,
        (shape((1, pairs), F32), shape((pushed, narrow), BF)),
        [vmem((2 * pushed, narrow), F32), vmem((pushed, narrow), F32)],
        1_200_000_000, 5_000_000,
        arrived, w_self, w_nbr, w_pair, w_out.reshape(1, -1), jnp.transpose(pair_slots),
        labels.reshape(1, pairs),
    )
    returned = lax.all_to_all(
        back.reshape(doms * subs, cap, narrow), both, 0, 0, tiled=True
    ).reshape(pushed, narrow)
    embed_grad = call(
        owner_kernel, shape((firms, narrow), F32), [vmem((pushed, narrow), F32)],
        2 * pushed * firms * narrow, 1_000_000, returned, push_t,
    )
    return (pair_loss.reshape(pairs), embed_grad)


def solution(mesh):
    in_specs = (
        P("dom", "sub"), P(), P(), P("dom", None, None), P("dom", None), P("dom"), P(), P(),
        P("dom", None, None, None), P(("dom", "sub"), None), P(("dom", "sub")),
    )
    out_specs = (P(("dom", "sub")), P("dom", "sub"))
    return jax.shard_map(
        per_device, mesh=mesh, in_specs=in_specs, out_specs=out_specs, check_vma=False
    )
```

```python
import jax
import jax.numpy as jnp
from jax import lax
from jax.experimental import pallas as pl
from jax.experimental.pallas import tpu as pltpu
from jax.sharding import PartitionSpec as P

BF = jnp.bfloat16
F32 = jnp.float32
DEAD = 4095
MIB = 1024 * 1024


def contract_first(a, b):
    return lax.dot_general(a, b, (((0,), (0,)), ((), ())), preferred_element_type=F32)


def call(kernel, out_shape, scratch, flops, nbytes, *args, in_specs=None, out_specs=None):
    where = {"hbm": pl.ANY, "vmem": pltpu.VMEM}
    specs = {}
    if in_specs is not None:
        args = [
            pltpu.with_memory_space_constraint(a, pltpu.HBM) if w[0] == "hbm" else a
            for a, w in zip(args, in_specs)
        ]
        specs["in_specs"] = [pl.BlockSpec(memory_space=where[w[-1]]) for w in in_specs]
    if out_specs is not None:
        specs["out_specs"] = [pl.BlockSpec(memory_space=where[w]) for w in out_specs]
    return pl.pallas_call(
        kernel,
        out_shape=out_shape,
        scratch_shapes=scratch,
        **specs,
        compiler_params=pltpu.CompilerParams(vmem_limit_bytes=24 * MIB),
        cost_estimate=pl.CostEstimate(flops=flops, bytes_accessed=nbytes, transcendentals=0),
    )(*args)


def one_hot_rows(columns, width):
    number = lax.broadcasted_iota(jnp.int32, (columns.shape[0], width), 1)
    return [
        jnp.where(columns[:, j : j + 1] == number, 1.0, 0.0).astype(BF)
        for j in range(columns.shape[1])
    ]


def halo_kernel(act_ref, rows_ref, out_ref, tmp_ref, pick_ref):
    slots, parts = rows_ref.shape
    for j, rows in enumerate(one_hot_rows(rows_ref[...].T, act_ref.shape[0])):
        pick_ref[j * parts : (j + 1) * parts, :] = rows
    picked = jnp.dot(pick_ref[...], act_ref[...], preferred_element_type=F32)
    for j in range(slots):
        tmp_ref[pl.ds(j, parts, stride=slots), :] = picked[j * parts : (j + 1) * parts]
    out_ref[...] = tmp_ref[...].astype(BF)


def count_kernel(
    act_ref, push_ref, nbr_ref, cnt_ref, near_ref, own_ref, actp_ref, cntp_ref,
    pick_ref, mine_ref, where_ref,
):
    groups, parts = push_ref.shape
    firms = act_ref.shape[0]
    degree = nbr_ref.shape[0]
    pushed = groups * parts
    i32, i16 = jnp.int32, jnp.int16
    for j, rows in enumerate(one_hot_rows(push_ref[...].T, firms)):
        pick_ref[j * parts : (j + 1) * parts, :] = rows
    pick = pick_ref[...]
    count = cnt_ref[...]
    live = lax.broadcasted_iota(i32, (degree, firms), 0) < count
    slot = jnp.where(live, nbr_ref[...], DEAD)
    counts = jnp.broadcast_to(count, (degree, firms))
    stack = jnp.concatenate([slot >> 7, slot & 127, counts], 0).astype(F32).astype(BF)
    chosen = lax.dot_general(
        pick, stack, (((1,), (1,)), ((), ())), preferred_element_type=F32
    )
    for j in range(groups):
        block = chosen[j * parts : (j + 1) * parts, 2 * degree : 3 * degree]
        cntp_ref[j : j + 1, :] = block.T[0:1, :]
    actp_ref[...] = jnp.dot(pick, act_ref[...], preferred_element_type=F32).astype(BF)
    batch = 16
    span = batch * degree
    shape = (2 * degree, 2 * span)
    lane = lax.broadcasted_iota(i32, shape, 1)
    spread = jnp.where(
        lax.broadcasted_iota(i32, shape, 0) == (lane // span) * degree + lane % degree, 1.0, 0.0
    ).astype(BF)
    wide = jnp.dot(chosen[:, : 2 * degree].astype(BF), spread, preferred_element_type=F32)
    row = lax.broadcasted_iota(i32, (pushed, 2 * span), 0) % batch
    lane = (lax.broadcasted_iota(i32, (pushed, 2 * span), 1) % span) // degree
    wide = jnp.where(row == lane, wide, 0.0).astype(BF)
    shape = (pushed // batch, pushed)
    gather = jnp.where(
        lax.broadcasted_iota(i32, shape, 1) // batch == lax.broadcasted_iota(i32, shape, 0), 1.0, 0.0
    ).astype(BF)
    where_ref[...] = jnp.dot(gather, wide, preferred_element_type=F32)
    own_row = (
        lax.broadcasted_iota(i32, (batch, span), 1) // degree
        == lax.broadcasted_iota(i32, (batch, span), 0)
    )
    low_number = lax.broadcasted_iota(i32, (128, span), 0).astype(i16)
    one = jnp.ones((batch, span), BF)
    zero = jnp.zeros((batch, span), BF)
    mine_blocks = firms // 128
    near_blocks = near_ref.shape[1] // 128

    def fill(g, carry):
        line = where_ref[pl.ds(g, 1), :]
        high = jnp.where(own_row, jnp.broadcast_to(line[:, :span], (batch, span)), -1.0)
        high = high.astype(i32).astype(i16)
        lhs = jnp.concatenate(
            [jnp.where(high == i16(h), one, zero) for h in range(mine_blocks + near_blocks)], 0
        )
        low = jnp.broadcast_to(line[:, span:], (128, span)).astype(i32).astype(i16)
        rhs = jnp.where(low == low_number, jnp.ones((128, span), BF), jnp.zeros((128, span), BF))
        counts = lax.dot_general(
            lhs, rhs, (((1,), (1,)), ((), ())), preferred_element_type=F32
        ).astype(BF)
        rows = pl.ds(pl.multiple_of(g * batch, batch), batch)
        for h in range(mine_blocks):
            mine_ref[rows, h * 128 : (h + 1) * 128] = counts[h * batch : (h + 1) * batch]
        for h in range(near_blocks):
            at = (mine_blocks + h) * batch
            near_ref[rows, h * 128 : (h + 1) * 128] = counts[at : at + batch]
        return carry

    lax.fori_loop(0, pushed // batch, fill, 0, unroll=4)
    own_ref[...] = jnp.dot(mine_ref[...], act_ref[...], preferred_element_type=F32)


def mean_kernel(halo_ref, near_ref, own_ref, actp_ref, cntp_ref, out_ref, tmp_ref):
    groups, parts = cntp_ref.shape
    divisor = cntp_ref[...].T
    summed = own_ref[...] + jnp.dot(near_ref[...], halo_ref[...], preferred_element_type=F32)

    def place(b, rows, kind):
        tmp_ref[pl.ds((b // 2) * 4 + kind * 2 + b % 2, parts, stride=2 * groups), :] = rows

    for b in range(groups):
        rows = slice(b * parts, (b + 1) * parts)
        place(b, actp_ref[rows, :].astype(F32), 0)
        mean = summed[rows] / divisor[:, b : b + 1]
        place(b, mean.astype(BF).astype(F32), 1)
    out_ref[...] = tmp_ref[...].astype(BF)


def decode_kernel(
    recv_ref, self_in, near_in, pair_in, wout_ref, slots_ref, label_ref,
    loss_ref, out_ref, tmp_ref, back_ref, self_ref, near_ref, pair_ref, sems,
):
    parts = recv_ref.shape[0] // 16
    pairs = slots_ref.shape[1]
    width = self_ref.shape[0]
    copies = [
        pltpu.make_async_copy(self_in, self_ref, sems.at[3]),
        pltpu.make_async_copy(near_in, near_ref, sems.at[4]),
    ]
    for i in range(3):
        rows = pl.ds(i * width, width)
        copies.append(pltpu.make_async_copy(pair_in.at[rows, :], pair_ref.at[rows, :], sems.at[i]))
    for copy in copies:
        copy.start()
    tmp_ref[...] = recv_ref[...].astype(F32)

    def rows_of(kind):
        halves = [
            jnp.concatenate(
                [
                    tmp_ref[pl.ds(s * 4 + kind * 2 + c, parts, stride=16), :]
                    for s in range(4)
                ],
                1,
            )
            for c in range(2)
        ]
        return jnp.concatenate(halves, 0).astype(BF)

    own, near = rows_of(0), rows_of(1)
    copies[0].wait()
    copies[1].wait()
    embed = (
        jnp.dot(own, self_ref[...], preferred_element_type=F32)
        + jnp.dot(near, near_ref[...], preferred_element_type=F32)
    ).astype(BF)
    place = lax.broadcasted_iota(jnp.int32, (2 * parts, pairs), 0)
    slot = jnp.where(place < parts, 2 * place, 2 * (place - parts) + 1)
    left_pick = jnp.where(slot == slots_ref[0:1, :], 1.0, 0.0).astype(BF)
    right_pick = jnp.where(slot == slots_ref[1:2, :], 1.0, 0.0).astype(BF)
    left = contract_first(left_pick, embed)
    right = contract_first(right_pick, embed)
    product = (left * right).astype(BF)
    pre_act = jnp.zeros((pairs, pair_ref.shape[1]), F32)
    for i, feature in enumerate((left.astype(BF), right.astype(BF), product)):
        copies[2 + i].wait()
        pre_act = pre_act + jnp.dot(
            feature, pair_ref[i * width : (i + 1) * width, :], preferred_element_type=F32
        )
    gate = jax.nn.sigmoid(pre_act)
    wout = wout_ref[...]
    logit = jnp.sum(pre_act * gate * wout, axis=1, keepdims=True)
    target = jnp.broadcast_to(label_ref[...].astype(F32), (pairs, pairs)).T[:, 0:1]
    loss = jnp.maximum(logit, 0.0) + jnp.log1p(jnp.exp(-jnp.abs(logit))) - target * logit
    loss_ref[...] = jnp.broadcast_to(loss, (pairs, pairs)).T[0:1, :]
    outer = jax.nn.sigmoid(logit) - target
    pre_grad = (outer * wout * gate * (1.0 + pre_act * (1.0 - gate))).astype(BF)
    feat = lax.dot_general(
        pre_grad, pair_ref[...], (((1,), (1,)), ((), ())), preferred_element_type=F32
    )
    third = feat[:, 2 * width :]
    left_grad = (feat[:, :width] + third * right).astype(BF)
    right_grad = (feat[:, width : 2 * width] + third * left).astype(BF)
    back = jnp.dot(left_pick, left_grad, preferred_element_type=F32) + jnp.dot(
        right_pick, right_grad, preferred_element_type=F32
    )
    for s in range(4):
        for c in range(2):
            back_ref[pl.ds(s * 2 + c, parts, stride=8), :] = back[
                c * parts : (c + 1) * parts, s * 128 : (s + 1) * 128
            ]
    out_ref[...] = back_ref[...].astype(BF)


def owner_kernel(recv_ref, push_ref, out_ref, tmp_ref):
    groups, parts = push_ref.shape
    tmp_ref[...] = recv_ref[...].astype(F32)
    grads = jnp.concatenate(
        [tmp_ref[pl.ds(b, parts, stride=groups), :] for b in range(groups)], 0
    ).astype(BF)
    firm = lax.broadcasted_iota(jnp.int32, (out_ref.shape[0], parts), 0)
    pick = jnp.concatenate(
        [
            jnp.where(firm == push_ref[b : b + 1, :], 1.0, 0.0).astype(BF)
            for b in range(groups)
        ],
        1,
    )
    out_ref[...] = jnp.dot(pick, grads, preferred_element_type=F32)


def per_device(
    firm_act, w_self, w_nbr, halo_rows, nbr_index, nbr_count, w_pair, w_out, push_rows,
    pair_slots, labels,
):
    firms, narrow = firm_act.shape
    doms, subs, cap = push_rows.shape[1:]
    slots = halo_rows.shape[2]
    both = ("dom", "sub")
    shape = jax.ShapeDtypeStruct
    vmem = pltpu.VMEM
    sems = pltpu.SemaphoreType.DMA
    halo_t = jnp.transpose(halo_rows[0])
    push_t = jnp.transpose(push_rows[0], (1, 2, 0)).reshape(subs * cap, doms)
    pushed = doms * subs * cap
    halos = doms * slots

    fetch = ("hbm", "vmem")
    outgoing = call(
        halo_kernel, shape((halos, narrow), BF),
        [vmem((halos, narrow), F32), vmem((halos, firms), BF)],
        2 * halos * firms * narrow, 600_000, firm_act, halo_t, in_specs=[fetch, fetch],
    )
    incoming = lax.all_to_all(
        outgoing.reshape(doms, slots, narrow), "dom", 0, 0, tiled=True
    ).reshape(halos, narrow)
    near_counts, own_sum, push_act, push_count = call(
        count_kernel,
        (
            shape((pushed, halos), BF), shape((pushed, narrow), F32), shape((pushed, narrow), BF),
            shape((subs * cap, doms), F32),
        ),
        [vmem((pushed, firms), BF), vmem((pushed, firms), BF), vmem((pushed // 16, 512), F32)],
        10_000_000_000, 4_000_000,
        firm_act, push_t, jnp.transpose(nbr_index), nbr_count.reshape(1, firms),
        in_specs=[fetch] * 4,
    )
    message = call(
        mean_kernel, shape((2 * pushed, narrow), BF), [vmem((2 * pushed, narrow), F32)],
        2 * halos * pushed * narrow, 4_000_000,
        incoming, near_counts, own_sum, push_act, push_count,
    )
    arrived = lax.all_to_all(
        message.reshape(doms * subs, 2 * cap, narrow), both, 0, 0, tiled=True
    ).reshape(2 * pushed, narrow)
    pairs = labels.shape[0]
    pair_loss, back = call(
        decode_kernel,
        (shape((1, pairs), F32), shape((pushed, narrow), BF)),
        [
            vmem((2 * pushed, narrow), F32), vmem((pushed, narrow), F32), vmem(w_self.shape, BF),
            vmem(w_nbr.shape, BF), vmem(w_pair.shape, BF), sems((5,)),
        ],
        1_200_000_000, 5_000_000,
        arrived, w_self, w_nbr, w_pair, w_out.reshape(1, -1), jnp.transpose(pair_slots),
        labels.reshape(1, pairs),
        in_specs=[("vmem",)] + [("hbm",)] * 3 + [("vmem",)] * 3,
    )
    returned = lax.all_to_all(
        back.reshape(doms * subs, cap, narrow), both, 0, 0, tiled=True
    ).reshape(pushed, narrow)
    embed_grad = call(
        owner_kernel, shape((firms, narrow), F32), [vmem((pushed, narrow), F32)],
        2 * pushed * firms * narrow, 1_000_000, returned, push_t,
    )
    return (pair_loss.reshape(pairs), embed_grad)


def solution(mesh):
    in_specs = (
        P("dom", "sub"), P(), P(), P("dom", None, None), P("dom", None), P("dom"), P(), P(),
        P("dom", None, None, None), P(("dom", "sub"), None), P(("dom", "sub")),
    )
    out_specs = (P(("dom", "sub")), P("dom", "sub"))
    return jax.shard_map(
        per_device, mesh=mesh, in_specs=in_specs, out_specs=out_specs, check_vma=False
    )
```

```python
import jax
import jax.numpy as jnp
from jax import lax
from jax.experimental import pallas as pl
from jax.experimental.pallas import tpu as pltpu
from jax.sharding import PartitionSpec as P

BF = jnp.bfloat16
F32 = jnp.float32
DEAD = 4095
MIB = 1024 * 1024


def contract_first(a, b):
    return lax.dot_general(a, b, (((0,), (0,)), ((), ())), preferred_element_type=F32)


def call(kernel, out_shape, scratch, flops, nbytes, *args, in_specs=None, out_specs=None, alias=None):
    where = {"hbm": pl.ANY, "vmem": pltpu.VMEM}
    specs = {}
    if in_specs is not None:
        args = [
            pltpu.with_memory_space_constraint(a, pltpu.HBM) if w[0] == "hbm" else a
            for a, w in zip(args, in_specs)
        ]
        specs["in_specs"] = [pl.BlockSpec(memory_space=where[w[-1]]) for w in in_specs]
    if out_specs is not None:
        specs["out_specs"] = [pl.BlockSpec(memory_space=where[w]) for w in out_specs]
    return pl.pallas_call(
        kernel,
        out_shape=out_shape,
        scratch_shapes=scratch,
        input_output_aliases=alias or {},
        **specs,
        compiler_params=pltpu.CompilerParams(vmem_limit_bytes=24 * MIB),
        cost_estimate=pl.CostEstimate(flops=flops, bytes_accessed=nbytes, transcendentals=0),
    )(*args)


def one_hot_rows(columns, width):
    number = lax.broadcasted_iota(jnp.int32, (columns.shape[0], width), 1)
    return [
        jnp.where(columns[:, j : j + 1] == number, 1.0, 0.0).astype(BF)
        for j in range(columns.shape[1])
    ]


def halo_kernel(act_ref, rows_ref, out_ref, tmp_ref, pick_ref):
    slots, parts = rows_ref.shape
    for j, rows in enumerate(one_hot_rows(rows_ref[...].T, act_ref.shape[0])):
        pick_ref[j * parts : (j + 1) * parts, :] = rows
    picked = jnp.dot(pick_ref[...], act_ref[...], preferred_element_type=F32)
    for j in range(slots):
        tmp_ref[pl.ds(j, parts, stride=slots), :] = picked[j * parts : (j + 1) * parts]
    out_ref[...] = tmp_ref[...].astype(BF)


def count_kernel(
    act_ref, push_ref, nbr_ref, cnt_ref, *refs
):
    weights, (near_ref, own_ref, actp_ref, cntp_ref), held = refs[:3], refs[3:7], refs[7:10]
    pick_ref, mine_ref, where_ref, sems = refs[10:]
    copies = [pltpu.make_async_copy(w, h, sems.at[i]) for i, (w, h) in enumerate(zip(weights, held))]
    for copy in copies:
        copy.start()
    groups, parts = push_ref.shape
    firms = act_ref.shape[0]
    degree = nbr_ref.shape[0]
    pushed = groups * parts
    i32, i16 = jnp.int32, jnp.int16
    for j, rows in enumerate(one_hot_rows(push_ref[...].T, firms)):
        pick_ref[j * parts : (j + 1) * parts, :] = rows
    pick = pick_ref[...]
    count = cnt_ref[...]
    live = lax.broadcasted_iota(i32, (degree, firms), 0) < count
    slot = jnp.where(live, nbr_ref[...], DEAD)
    counts = jnp.broadcast_to(count, (degree, firms))
    stack = jnp.concatenate([slot >> 7, slot & 127, counts], 0).astype(F32).astype(BF)
    chosen = lax.dot_general(
        pick, stack, (((1,), (1,)), ((), ())), preferred_element_type=F32
    )
    for j in range(groups):
        block = chosen[j * parts : (j + 1) * parts, 2 * degree : 3 * degree]
        cntp_ref[j : j + 1, :] = block.T[0:1, :]
    actp_ref[...] = jnp.dot(pick, act_ref[...], preferred_element_type=F32).astype(BF)
    batch = 16
    span = batch * degree
    shape = (2 * degree, 2 * span)
    lane = lax.broadcasted_iota(i32, shape, 1)
    spread = jnp.where(
        lax.broadcasted_iota(i32, shape, 0) == (lane // span) * degree + lane % degree, 1.0, 0.0
    ).astype(BF)
    wide = jnp.dot(chosen[:, : 2 * degree].astype(BF), spread, preferred_element_type=F32)
    row = lax.broadcasted_iota(i32, (pushed, 2 * span), 0) % batch
    lane = (lax.broadcasted_iota(i32, (pushed, 2 * span), 1) % span) // degree
    wide = jnp.where(row == lane, wide, 0.0).astype(BF)
    shape = (pushed // batch, pushed)
    gather = jnp.where(
        lax.broadcasted_iota(i32, shape, 1) // batch == lax.broadcasted_iota(i32, shape, 0), 1.0, 0.0
    ).astype(BF)
    where_ref[...] = jnp.dot(gather, wide, preferred_element_type=F32)
    own_row = (
        lax.broadcasted_iota(i32, (batch, span), 1) // degree
        == lax.broadcasted_iota(i32, (batch, span), 0)
    )
    low_number = lax.broadcasted_iota(i32, (128, span), 0).astype(i16)
    one = jnp.ones((batch, span), BF)
    zero = jnp.zeros((batch, span), BF)
    mine_blocks = firms // 128
    near_blocks = near_ref.shape[1] // 128

    def fill(g, carry):
        line = where_ref[pl.ds(g, 1), :]
        high = jnp.where(own_row, jnp.broadcast_to(line[:, :span], (batch, span)), -1.0)
        high = high.astype(i32).astype(i16)
        lhs = jnp.concatenate(
            [jnp.where(high == i16(h), one, zero) for h in range(mine_blocks + near_blocks)], 0
        )
        low = jnp.broadcast_to(line[:, span:], (128, span)).astype(i32).astype(i16)
        rhs = jnp.where(low == low_number, jnp.ones((128, span), BF), jnp.zeros((128, span), BF))
        counts = lax.dot_general(
            lhs, rhs, (((1,), (1,)), ((), ())), preferred_element_type=F32
        ).astype(BF)
        rows = pl.ds(pl.multiple_of(g * batch, batch), batch)
        for h in range(mine_blocks):
            mine_ref[rows, h * 128 : (h + 1) * 128] = counts[h * batch : (h + 1) * batch]
        for h in range(near_blocks):
            at = (mine_blocks + h) * batch
            near_ref[rows, h * 128 : (h + 1) * 128] = counts[at : at + batch]
        return carry

    lax.fori_loop(0, pushed // batch, fill, 0, unroll=4)
    own_ref[...] = jnp.dot(mine_ref[...], act_ref[...], preferred_element_type=F32)
    for copy in copies:
        copy.wait()


def mean_kernel(halo_ref, near_ref, own_ref, actp_ref, cntp_ref, *refs):
    out_ref, tmp_ref = refs[3], refs[7]
    groups, parts = cntp_ref.shape
    divisor = cntp_ref[...].T
    summed = own_ref[...] + jnp.dot(near_ref[...], halo_ref[...], preferred_element_type=F32)

    def place(b, rows, kind):
        tmp_ref[pl.ds((b // 2) * 4 + kind * 2 + b % 2, parts, stride=2 * groups), :] = rows

    for b in range(groups):
        rows = slice(b * parts, (b + 1) * parts)
        place(b, actp_ref[rows, :].astype(F32), 0)
        mean = summed[rows] / divisor[:, b : b + 1]
        place(b, mean.astype(BF).astype(F32), 1)
    out_ref[...] = tmp_ref[...].astype(BF)


def decode_kernel(
    recv_ref, self_ref, near_ref, pair_ref, wout_ref, slots_ref, label_ref,
    loss_ref, out_ref, tmp_ref, back_ref,
):
    parts = recv_ref.shape[0] // 16
    pairs = slots_ref.shape[1]
    width = self_ref.shape[0]
    tmp_ref[...] = recv_ref[...].astype(F32)

    def rows_of(kind):
        halves = [
            jnp.concatenate(
                [
                    tmp_ref[pl.ds(s * 4 + kind * 2 + c, parts, stride=16), :]
                    for s in range(4)
                ],
                1,
            )
            for c in range(2)
        ]
        return jnp.concatenate(halves, 0).astype(BF)

    own, near = rows_of(0), rows_of(1)
    embed = (
        jnp.dot(own, self_ref[...], preferred_element_type=F32)
        + jnp.dot(near, near_ref[...], preferred_element_type=F32)
    ).astype(BF)
    place = lax.broadcasted_iota(jnp.int32, (2 * parts, pairs), 0)
    slot = jnp.where(place < parts, 2 * place, 2 * (place - parts) + 1)
    left_pick = jnp.where(slot == slots_ref[0:1, :], 1.0, 0.0).astype(BF)
    right_pick = jnp.where(slot == slots_ref[1:2, :], 1.0, 0.0).astype(BF)
    left = contract_first(left_pick, embed)
    right = contract_first(right_pick, embed)
    product = (left * right).astype(BF)
    pre_act = jnp.zeros((pairs, pair_ref.shape[1]), F32)
    for i, feature in enumerate((left.astype(BF), right.astype(BF), product)):
        pre_act = pre_act + jnp.dot(
            feature, pair_ref[i * width : (i + 1) * width, :], preferred_element_type=F32
        )
    gate = jax.nn.sigmoid(pre_act)
    wout = wout_ref[...]
    logit = jnp.sum(pre_act * gate * wout, axis=1, keepdims=True)
    target = jnp.broadcast_to(label_ref[...].astype(F32), (pairs, pairs)).T[:, 0:1]
    loss = jnp.maximum(logit, 0.0) + jnp.log1p(jnp.exp(-jnp.abs(logit))) - target * logit
    loss_ref[...] = jnp.broadcast_to(loss, (pairs, pairs)).T[0:1, :]
    outer = jax.nn.sigmoid(logit) - target
    pre_grad = (outer * wout * gate * (1.0 + pre_act * (1.0 - gate))).astype(BF)
    feat = lax.dot_general(
        pre_grad, pair_ref[...], (((1,), (1,)), ((), ())), preferred_element_type=F32
    )
    third = feat[:, 2 * width :]
    left_grad = (feat[:, :width] + third * right).astype(BF)
    right_grad = (feat[:, width : 2 * width] + third * left).astype(BF)
    back = jnp.dot(left_pick, left_grad, preferred_element_type=F32) + jnp.dot(
        right_pick, right_grad, preferred_element_type=F32
    )
    for s in range(4):
        for c in range(2):
            back_ref[pl.ds(s * 2 + c, parts, stride=8), :] = back[
                c * parts : (c + 1) * parts, s * 128 : (s + 1) * 128
            ]
    out_ref[...] = back_ref[...].astype(BF)


def owner_kernel(recv_ref, push_ref, out_ref, tmp_ref):
    groups, parts = push_ref.shape
    tmp_ref[...] = recv_ref[...].astype(F32)
    grads = jnp.concatenate(
        [tmp_ref[pl.ds(b, parts, stride=groups), :] for b in range(groups)], 0
    ).astype(BF)
    firm = lax.broadcasted_iota(jnp.int32, (out_ref.shape[0], parts), 0)
    pick = jnp.concatenate(
        [
            jnp.where(firm == push_ref[b : b + 1, :], 1.0, 0.0).astype(BF)
            for b in range(groups)
        ],
        1,
    )
    out_ref[...] = jnp.dot(pick, grads, preferred_element_type=F32)


def per_device(
    firm_act, w_self, w_nbr, halo_rows, nbr_index, nbr_count, w_pair, w_out, push_rows,
    pair_slots, labels,
):
    firms, narrow = firm_act.shape
    doms, subs, cap = push_rows.shape[1:]
    slots = halo_rows.shape[2]
    both = ("dom", "sub")
    shape = jax.ShapeDtypeStruct
    vmem = pltpu.VMEM
    sems = pltpu.SemaphoreType.DMA
    halo_t = jnp.transpose(halo_rows[0])
    push_t = jnp.transpose(push_rows[0], (1, 2, 0)).reshape(subs * cap, doms)
    pushed = doms * subs * cap
    halos = doms * slots

    fetch = ("hbm", "vmem")
    outgoing = call(
        halo_kernel, shape((halos, narrow), BF),
        [vmem((halos, narrow), F32), vmem((halos, firms), BF)],
        2 * halos * firms * narrow, 600_000, firm_act, halo_t, in_specs=[fetch, fetch],
    )
    incoming = lax.all_to_all(
        outgoing.reshape(doms, slots, narrow), "dom", 0, 0, tiled=True
    ).reshape(halos, narrow)
    weights = (w_self, w_nbr, w_pair)
    held = tuple(pltpu.HBM(w.shape, w.dtype) for w in weights)
    near_counts, own_sum, push_act, push_count, *copied = call(
        count_kernel,
        (
            shape((pushed, halos), BF), shape((pushed, narrow), F32), shape((pushed, narrow), BF),
            shape((subs * cap, doms), F32), *held,
        ),
        [
            vmem((pushed, firms), BF), vmem((pushed, firms), BF), vmem((pushed // 16, 512), F32),
            sems((3,)),
        ],
        10_000_000_000, 4_000_000,
        firm_act, push_t, jnp.transpose(nbr_index), nbr_count.reshape(1, firms),
        *weights, in_specs=[fetch] * 4 + [("hbm",)] * 3, out_specs=["vmem"] * 4 + ["hbm"] * 3,
    )
    message, w_self, w_nbr, w_pair = call(
        mean_kernel, (shape((2 * pushed, narrow), BF), *held), [vmem((2 * pushed, narrow), F32)],
        2 * halos * pushed * narrow, 4_000_000,
        incoming, near_counts, own_sum, push_act, push_count, *copied,
        in_specs=[("vmem",)] * 5 + [("hbm",)] * 3, out_specs=["vmem"] + ["hbm"] * 3,
        alias={5: 1, 6: 2, 7: 3},
    )
    arrived = lax.all_to_all(
        message.reshape(doms * subs, 2 * cap, narrow), both, 0, 0, tiled=True
    ).reshape(2 * pushed, narrow)
    pairs = labels.shape[0]
    pair_loss, back = call(
        decode_kernel,
        (shape((1, pairs), F32), shape((pushed, narrow), BF)),
        [vmem((2 * pushed, narrow), F32), vmem((pushed, narrow), F32)],
        1_200_000_000, 5_000_000,
        arrived, w_self, w_nbr, w_pair, w_out.reshape(1, -1), jnp.transpose(pair_slots),
        labels.reshape(1, pairs),
    )
    returned = lax.all_to_all(
        back.reshape(doms * subs, cap, narrow), both, 0, 0, tiled=True
    ).reshape(pushed, narrow)
    embed_grad = call(
        owner_kernel, shape((firms, narrow), F32), [vmem((pushed, narrow), F32)],
        2 * pushed * firms * narrow, 1_000_000, returned, push_t,
    )
    return (pair_loss.reshape(pairs), embed_grad)


def solution(mesh):
    in_specs = (
        P("dom", "sub"), P(), P(), P("dom", None, None), P("dom", None), P("dom"), P(), P(),
        P("dom", None, None, None), P(("dom", "sub"), None), P(("dom", "sub")),
    )
    out_specs = (P(("dom", "sub")), P("dom", "sub"))
    return jax.shard_map(
        per_device, mesh=mesh, in_specs=in_specs, out_specs=out_specs, check_vma=False
    )
```

```python
import jax
import jax.numpy as jnp
from jax import lax
from jax.experimental import pallas as pl
from jax.experimental.pallas import tpu as pltpu
from jax.sharding import PartitionSpec as P

BF = jnp.bfloat16
F32 = jnp.float32
DEAD = 4095
MIB = 1024 * 1024


def contract_first(a, b):
    return lax.dot_general(a, b, (((0,), (0,)), ((), ())), preferred_element_type=F32)


def call(kernel, out_shape, scratch, flops, nbytes, *args, in_specs=None, out_specs=None):
    where = {"hbm": pl.ANY, "vmem": pltpu.VMEM}
    specs = {}
    if in_specs is not None:
        args = [
            pltpu.with_memory_space_constraint(a, pltpu.HBM) if w[0] == "hbm" else a
            for a, w in zip(args, in_specs)
        ]
        specs["in_specs"] = [pl.BlockSpec(memory_space=where[w[-1]]) for w in in_specs]
    if out_specs is not None:
        specs["out_specs"] = [pl.BlockSpec(memory_space=where[w]) for w in out_specs]
        if len(out_specs) == 1:
            specs["out_specs"] = specs["out_specs"][0]
    return pl.pallas_call(
        kernel,
        out_shape=out_shape,
        scratch_shapes=scratch,
        **specs,
        compiler_params=pltpu.CompilerParams(vmem_limit_bytes=24 * MIB),
        cost_estimate=pl.CostEstimate(flops=flops, bytes_accessed=nbytes, transcendentals=0),
    )(*args)


def one_hot_rows(columns, width):
    number = lax.broadcasted_iota(jnp.int32, (columns.shape[0], width), 1)
    return [
        jnp.where(columns[:, j : j + 1] == number, 1.0, 0.0).astype(BF)
        for j in range(columns.shape[1])
    ]


def halo_kernel(act_ref, rows_ref, out_ref, tmp_ref, pick_ref):
    slots, parts = rows_ref.shape
    for j, rows in enumerate(one_hot_rows(rows_ref[...].T, act_ref.shape[0])):
        pick_ref[j * parts : (j + 1) * parts, :] = rows
    picked = jnp.dot(pick_ref[...], act_ref[...], preferred_element_type=F32)
    for j in range(slots):
        tmp_ref[pl.ds(j, parts, stride=slots), :] = picked[j * parts : (j + 1) * parts]
    out_ref[...] = tmp_ref[...].astype(BF)


def count_kernel(
    act_ref, push_ref, nbr_ref, cnt_ref, near_ref, own_ref, actp_ref, cntp_ref,
    pick_ref, mine_ref, where_ref,
):
    groups, parts = push_ref.shape
    firms = act_ref.shape[0]
    degree = nbr_ref.shape[0]
    pushed = groups * parts
    i32, i16 = jnp.int32, jnp.int16
    for j, rows in enumerate(one_hot_rows(push_ref[...].T, firms)):
        pick_ref[j * parts : (j + 1) * parts, :] = rows
    pick = pick_ref[...]
    count = cnt_ref[...]
    live = lax.broadcasted_iota(i32, (degree, firms), 0) < count
    slot = jnp.where(live, nbr_ref[...], DEAD)
    counts = jnp.broadcast_to(count, (degree, firms))
    stack = jnp.concatenate([slot >> 7, slot & 127, counts], 0).astype(F32).astype(BF)
    chosen = lax.dot_general(
        pick, stack, (((1,), (1,)), ((), ())), preferred_element_type=F32
    )
    for j in range(groups):
        block = chosen[j * parts : (j + 1) * parts, 2 * degree : 3 * degree]
        cntp_ref[j : j + 1, :] = block.T[0:1, :]
    actp_ref[...] = jnp.dot(pick, act_ref[...], preferred_element_type=F32).astype(BF)
    batch = 16
    span = batch * degree
    shape = (2 * degree, 2 * span)
    lane = lax.broadcasted_iota(i32, shape, 1)
    spread = jnp.where(
        lax.broadcasted_iota(i32, shape, 0) == (lane // span) * degree + lane % degree, 1.0, 0.0
    ).astype(BF)
    wide = jnp.dot(chosen[:, : 2 * degree].astype(BF), spread, preferred_element_type=F32)
    row = lax.broadcasted_iota(i32, (pushed, 2 * span), 0) % batch
    lane = (lax.broadcasted_iota(i32, (pushed, 2 * span), 1) % span) // degree
    wide = jnp.where(row == lane, wide, 0.0).astype(BF)
    shape = (pushed // batch, pushed)
    gather = jnp.where(
        lax.broadcasted_iota(i32, shape, 1) // batch == lax.broadcasted_iota(i32, shape, 0), 1.0, 0.0
    ).astype(BF)
    where_ref[...] = jnp.dot(gather, wide, preferred_element_type=F32)
    own_row = (
        lax.broadcasted_iota(i32, (batch, span), 1) // degree
        == lax.broadcasted_iota(i32, (batch, span), 0)
    )
    low_number = lax.broadcasted_iota(i32, (128, span), 0).astype(i16)
    one = jnp.ones((batch, span), BF)
    zero = jnp.zeros((batch, span), BF)
    mine_blocks = firms // 128
    near_blocks = near_ref.shape[1] // 128

    def fill(g, carry):
        line = where_ref[pl.ds(g, 1), :]
        high = jnp.where(own_row, jnp.broadcast_to(line[:, :span], (batch, span)), -1.0)
        high = high.astype(i32).astype(i16)
        lhs = jnp.concatenate(
            [jnp.where(high == i16(h), one, zero) for h in range(mine_blocks + near_blocks)], 0
        )
        low = jnp.broadcast_to(line[:, span:], (128, span)).astype(i32).astype(i16)
        rhs = jnp.where(low == low_number, jnp.ones((128, span), BF), jnp.zeros((128, span), BF))
        counts = lax.dot_general(
            lhs, rhs, (((1,), (1,)), ((), ())), preferred_element_type=F32
        ).astype(BF)
        rows = pl.ds(pl.multiple_of(g * batch, batch), batch)
        for h in range(mine_blocks):
            mine_ref[rows, h * 128 : (h + 1) * 128] = counts[h * batch : (h + 1) * batch]
        for h in range(near_blocks):
            at = (mine_blocks + h) * batch
            near_ref[rows, h * 128 : (h + 1) * 128] = counts[at : at + batch]
        return carry

    lax.fori_loop(0, pushed // batch, fill, 0, unroll=4)
    own_ref[...] = jnp.dot(mine_ref[...], act_ref[...], preferred_element_type=F32)


def mean_kernel(
    halo_ref, near_ref, own_ref, actp_ref, cntp_ref, self_in, nbr_in, pair_in,
    out_ref, self_ref, nbr_ref, pair_ref, tmp_ref, sems,
):
    copies = [
        pltpu.make_async_copy(self_in, self_ref, sems.at[0]),
        pltpu.make_async_copy(nbr_in, nbr_ref, sems.at[1]),
        pltpu.make_async_copy(pair_in.at[pl.ds(0, pair_ref.shape[0]), :], pair_ref, sems.at[2]),
    ]
    for copy in copies:
        copy.start()
    groups, parts = cntp_ref.shape
    divisor = cntp_ref[...].T
    summed = own_ref[...] + jnp.dot(near_ref[...], halo_ref[...], preferred_element_type=F32)

    def place(b, rows, kind):
        tmp_ref[pl.ds((b // 2) * 4 + kind * 2 + b % 2, parts, stride=2 * groups), :] = rows

    for b in range(groups):
        rows = slice(b * parts, (b + 1) * parts)
        place(b, actp_ref[rows, :].astype(F32), 0)
        mean = summed[rows] / divisor[:, b : b + 1]
        place(b, mean.astype(BF).astype(F32), 1)
    out_ref[...] = tmp_ref[...].astype(BF)
    for copy in copies:
        copy.wait()


def decode_kernel(
    recv_ref, self_ref, near_ref, first_ref, pair_in, wout_ref, slots_ref, label_ref,
    loss_ref, out_ref, tmp_ref, back_ref, rest_ref, sems,
):
    parts = recv_ref.shape[0] // 16
    pairs = slots_ref.shape[1]
    width = self_ref.shape[0]
    copies = []
    for i in range(2):
        rows = pl.ds(i * width, width)
        copies.append(
            pltpu.make_async_copy(
                pair_in.at[pl.ds((i + 1) * width, width), :], rest_ref.at[rows, :], sems.at[i]
            )
        )
        copies[-1].start()
    tmp_ref[...] = recv_ref[...].astype(F32)

    def rows_of(kind):
        halves = [
            jnp.concatenate(
                [
                    tmp_ref[pl.ds(s * 4 + kind * 2 + c, parts, stride=16), :]
                    for s in range(4)
                ],
                1,
            )
            for c in range(2)
        ]
        return jnp.concatenate(halves, 0).astype(BF)

    own, near = rows_of(0), rows_of(1)
    embed = (
        jnp.dot(own, self_ref[...], preferred_element_type=F32)
        + jnp.dot(near, near_ref[...], preferred_element_type=F32)
    ).astype(BF)
    place = lax.broadcasted_iota(jnp.int32, (2 * parts, pairs), 0)
    slot = jnp.where(place < parts, 2 * place, 2 * (place - parts) + 1)
    left_pick = jnp.where(slot == slots_ref[0:1, :], 1.0, 0.0).astype(BF)
    right_pick = jnp.where(slot == slots_ref[1:2, :], 1.0, 0.0).astype(BF)
    left = contract_first(left_pick, embed)
    right = contract_first(right_pick, embed)
    product = (left * right).astype(BF)
    pre_act = jnp.dot(left.astype(BF), first_ref[...], preferred_element_type=F32)
    for i, feature in enumerate((right.astype(BF), product)):
        copies[i].wait()
        pre_act = pre_act + jnp.dot(
            feature, rest_ref[i * width : (i + 1) * width, :], preferred_element_type=F32
        )
    gate = jax.nn.sigmoid(pre_act)
    wout = wout_ref[...]
    logit = jnp.sum(pre_act * gate * wout, axis=1, keepdims=True)
    target = jnp.broadcast_to(label_ref[...].astype(F32), (pairs, pairs)).T[:, 0:1]
    loss = jnp.maximum(logit, 0.0) + jnp.log1p(jnp.exp(-jnp.abs(logit))) - target * logit
    loss_ref[...] = jnp.broadcast_to(loss, (pairs, pairs)).T[0:1, :]
    outer = jax.nn.sigmoid(logit) - target
    pre_grad = (outer * wout * gate * (1.0 + pre_act * (1.0 - gate))).astype(BF)

    def back_through(weights):
        return lax.dot_general(
            pre_grad, weights, (((1,), (1,)), ((), ())), preferred_element_type=F32
        )

    feat = back_through(rest_ref[...])
    third = feat[:, width:]
    left_grad = (back_through(first_ref[...]) + third * right).astype(BF)
    right_grad = (feat[:, :width] + third * left).astype(BF)
    back = jnp.dot(left_pick, left_grad, preferred_element_type=F32) + jnp.dot(
        right_pick, right_grad, preferred_element_type=F32
    )
    for s in range(4):
        for c in range(2):
            back_ref[pl.ds(s * 2 + c, parts, stride=8), :] = back[
                c * parts : (c + 1) * parts, s * 128 : (s + 1) * 128
            ]
    out_ref[...] = back_ref[...].astype(BF)


def owner_kernel(recv_ref, push_ref, out_ref, tmp_ref):
    groups, parts = push_ref.shape
    tmp_ref[...] = recv_ref[...].astype(F32)
    grads = jnp.concatenate(
        [tmp_ref[pl.ds(b, parts, stride=groups), :] for b in range(groups)], 0
    ).astype(BF)
    firm = lax.broadcasted_iota(jnp.int32, (out_ref.shape[0], parts), 0)
    pick = jnp.concatenate(
        [
            jnp.where(firm == push_ref[b : b + 1, :], 1.0, 0.0).astype(BF)
            for b in range(groups)
        ],
        1,
    )
    out_ref[...] = jnp.dot(pick, grads, preferred_element_type=F32)


def per_device(
    firm_act, w_self, w_nbr, halo_rows, nbr_index, nbr_count, w_pair, w_out, push_rows,
    pair_slots, labels,
):
    firms, narrow = firm_act.shape
    doms, subs, cap = push_rows.shape[1:]
    slots = halo_rows.shape[2]
    both = ("dom", "sub")
    shape = jax.ShapeDtypeStruct
    vmem = pltpu.VMEM
    sems = pltpu.SemaphoreType.DMA
    halo_t = jnp.transpose(halo_rows[0])
    push_t = jnp.transpose(push_rows[0], (1, 2, 0)).reshape(subs * cap, doms)
    pushed = doms * subs * cap
    halos = doms * slots

    fetch = ("hbm", "vmem")
    outgoing = call(
        halo_kernel, shape((halos, narrow), BF),
        [vmem((halos, narrow), F32), vmem((halos, firms), BF)],
        2 * halos * firms * narrow, 600_000, firm_act, halo_t, in_specs=[fetch, fetch],
    )
    incoming = lax.all_to_all(
        outgoing.reshape(doms, slots, narrow), "dom", 0, 0, tiled=True
    ).reshape(halos, narrow)
    near_counts, own_sum, push_act, push_count = call(
        count_kernel,
        (
            shape((pushed, halos), BF), shape((pushed, narrow), F32), shape((pushed, narrow), BF),
            shape((subs * cap, doms), F32),
        ),
        [vmem((pushed, firms), BF), vmem((pushed, firms), BF), vmem((pushed // 16, 512), F32)],
        10_000_000_000, 4_000_000,
        firm_act, push_t, jnp.transpose(nbr_index), nbr_count.reshape(1, firms),
        in_specs=[fetch] * 4,
    )
    first = shape((w_self.shape[1], w_pair.shape[1]), BF)
    message, self_here, nbr_here, first_here = call(
        mean_kernel,
        (shape((2 * pushed, narrow), BF), shape(w_self.shape, BF), shape(w_nbr.shape, BF), first),
        [vmem((2 * pushed, narrow), F32), sems((3,))],
        2 * halos * pushed * narrow, 4_000_000,
        incoming, near_counts, own_sum, push_act, push_count, w_self, w_nbr, w_pair,
        in_specs=[("vmem",)] * 5 + [("hbm",)] * 3,
    )
    arrived = lax.all_to_all(
        message.reshape(doms * subs, 2 * cap, narrow), both, 0, 0, tiled=True
    ).reshape(2 * pushed, narrow)
    pairs = labels.shape[0]
    pair_loss, back = call(
        decode_kernel,
        (shape((1, pairs), F32), shape((pushed, narrow), BF)),
        [
            vmem((2 * pushed, narrow), F32), vmem((pushed, narrow), F32),
            vmem((w_pair.shape[0] - first.shape[0], w_pair.shape[1]), BF), sems((2,)),
        ],
        1_200_000_000, 5_000_000,
        arrived, self_here, nbr_here, first_here, w_pair, w_out.reshape(1, -1), jnp.transpose(pair_slots),
        labels.reshape(1, pairs),
        in_specs=[("vmem",)] * 4 + [("hbm",)] + [("vmem",)] * 3,
    )
    returned = lax.all_to_all(
        back.reshape(doms * subs, cap, narrow), both, 0, 0, tiled=True
    ).reshape(pushed, narrow)
    embed_grad = call(
        owner_kernel, shape((firms, narrow), F32), [vmem((pushed, narrow), F32)],
        2 * pushed * firms * narrow, 1_000_000, returned, push_t,
    )
    return (pair_loss.reshape(pairs), embed_grad)


def solution(mesh):
    in_specs = (
        P("dom", "sub"), P(), P(), P("dom", None, None), P("dom", None), P("dom"), P(), P(),
        P("dom", None, None, None), P(("dom", "sub"), None), P(("dom", "sub")),
    )
    out_specs = (P(("dom", "sub")), P("dom", "sub"))
    return jax.shard_map(
        per_device, mesh=mesh, in_specs=in_specs, out_specs=out_specs, check_vma=False
    )
```

```python
import jax
import jax.numpy as jnp
from jax import lax
from jax.experimental import pallas as pl
from jax.experimental.pallas import tpu as pltpu
from jax.sharding import PartitionSpec as P

BF = jnp.bfloat16
F32 = jnp.float32
DEAD = 4095
MIB = 1024 * 1024


def contract_first(a, b):
    return lax.dot_general(a, b, (((0,), (0,)), ((), ())), preferred_element_type=F32)


def call(kernel, out_shape, scratch, flops, nbytes, *args, in_specs=None, out_specs=None):
    where = {"hbm": pl.ANY, "vmem": pltpu.VMEM}
    specs = {}
    if in_specs is not None:
        args = [
            pltpu.with_memory_space_constraint(a, pltpu.HBM) if w[0] == "hbm" else a
            for a, w in zip(args, in_specs)
        ]
        specs["in_specs"] = [pl.BlockSpec(memory_space=where[w[-1]]) for w in in_specs]
    if out_specs is not None:
        specs["out_specs"] = [pl.BlockSpec(memory_space=where[w]) for w in out_specs]
    return pl.pallas_call(
        kernel,
        out_shape=out_shape,
        scratch_shapes=scratch,
        **specs,
        compiler_params=pltpu.CompilerParams(vmem_limit_bytes=24 * MIB),
        cost_estimate=pl.CostEstimate(flops=flops, bytes_accessed=nbytes, transcendentals=0),
    )(*args)


def one_hot_rows(columns, width):
    number = lax.broadcasted_iota(jnp.int32, (columns.shape[0], width), 1)
    return [
        jnp.where(columns[:, j : j + 1] == number, 1.0, 0.0).astype(BF)
        for j in range(columns.shape[1])
    ]


def halo_kernel(act_ref, rows_ref, out_ref, tmp_ref, pick_ref):
    slots, parts = rows_ref.shape
    for j, rows in enumerate(one_hot_rows(rows_ref[...].T, act_ref.shape[0])):
        pick_ref[j * parts : (j + 1) * parts, :] = rows
    picked = jnp.dot(pick_ref[...], act_ref[...], preferred_element_type=F32)
    for j in range(slots):
        tmp_ref[pl.ds(j, parts, stride=slots), :] = picked[j * parts : (j + 1) * parts]
    out_ref[...] = tmp_ref[...].astype(BF)


def count_kernel(
    act_ref, push_ref, nbr_ref, cnt_ref, near_ref, own_ref, actp_ref, cntp_ref,
    pick_ref, mine_ref, where_ref,
):
    groups, parts = push_ref.shape
    firms = act_ref.shape[0]
    degree = nbr_ref.shape[0]
    pushed = groups * parts
    i32, i16 = jnp.int32, jnp.int16
    for j, rows in enumerate(one_hot_rows(push_ref[...].T, firms)):
        pick_ref[j * parts : (j + 1) * parts, :] = rows
    pick = pick_ref[...]
    count = cnt_ref[...]
    live = lax.broadcasted_iota(i32, (degree, firms), 0) < count
    slot = jnp.where(live, nbr_ref[...], DEAD)
    counts = jnp.broadcast_to(count, (degree, firms))
    stack = jnp.concatenate([slot >> 7, slot & 127, counts], 0).astype(F32).astype(BF)
    chosen = lax.dot_general(
        pick, stack, (((1,), (1,)), ((), ())), preferred_element_type=F32
    )
    for j in range(groups):
        block = chosen[j * parts : (j + 1) * parts, 2 * degree : 3 * degree]
        cntp_ref[j : j + 1, :] = block.T[0:1, :]
    actp_ref[...] = jnp.dot(pick, act_ref[...], preferred_element_type=F32).astype(BF)
    batch = 16
    span = batch * degree
    shape = (2 * degree, 2 * span)
    lane = lax.broadcasted_iota(i32, shape, 1)
    spread = jnp.where(
        lax.broadcasted_iota(i32, shape, 0) == (lane // span) * degree + lane % degree, 1.0, 0.0
    ).astype(BF)
    wide = jnp.dot(chosen[:, : 2 * degree].astype(BF), spread, preferred_element_type=F32)
    row = lax.broadcasted_iota(i32, (pushed, 2 * span), 0) % batch
    lane = (lax.broadcasted_iota(i32, (pushed, 2 * span), 1) % span) // degree
    wide = jnp.where(row == lane, wide, 0.0).astype(BF)
    shape = (pushed // batch, pushed)
    gather = jnp.where(
        lax.broadcasted_iota(i32, shape, 1) // batch == lax.broadcasted_iota(i32, shape, 0), 1.0, 0.0
    ).astype(BF)
    where_ref[...] = jnp.dot(gather, wide, preferred_element_type=F32)
    own_row = (
        lax.broadcasted_iota(i32, (batch, span), 1) // degree
        == lax.broadcasted_iota(i32, (batch, span), 0)
    )
    low_number = lax.broadcasted_iota(i32, (128, span), 0).astype(i16)
    one = jnp.ones((batch, span), BF)
    zero = jnp.zeros((batch, span), BF)
    mine_blocks = firms // 128
    near_blocks = near_ref.shape[1] // 128

    def fill(g, carry):
        line = where_ref[pl.ds(g, 1), :]
        high = jnp.where(own_row, jnp.broadcast_to(line[:, :span], (batch, span)), -1.0)
        high = high.astype(i32).astype(i16)
        lhs = jnp.concatenate(
            [jnp.where(high == i16(h), one, zero) for h in range(mine_blocks + near_blocks)], 0
        )
        low = jnp.broadcast_to(line[:, span:], (128, span)).astype(i32).astype(i16)
        rhs = jnp.where(low == low_number, jnp.ones((128, span), BF), jnp.zeros((128, span), BF))
        counts = lax.dot_general(
            lhs, rhs, (((1,), (1,)), ((), ())), preferred_element_type=F32
        ).astype(BF)
        rows = pl.ds(pl.multiple_of(g * batch, batch), batch)
        for h in range(mine_blocks):
            mine_ref[rows, h * 128 : (h + 1) * 128] = counts[h * batch : (h + 1) * batch]
        for h in range(near_blocks):
            at = (mine_blocks + h) * batch
            near_ref[rows, h * 128 : (h + 1) * 128] = counts[at : at + batch]
        return carry

    lax.fori_loop(0, pushed // batch, fill, 0, unroll=4)
    own_ref[...] = jnp.dot(mine_ref[...], act_ref[...], preferred_element_type=F32)


def mean_kernel(halo_ref, near_ref, own_ref, actp_ref, cntp_ref, out_ref, tmp_ref):
    groups, parts = cntp_ref.shape
    divisor = cntp_ref[...].T
    summed = own_ref[...] + jnp.dot(near_ref[...], halo_ref[...], preferred_element_type=F32)

    def place(b, rows, kind):
        tmp_ref[pl.ds((b // 2) * 4 + kind * 2 + b % 2, parts, stride=2 * groups), :] = rows

    for b in range(groups):
        rows = slice(b * parts, (b + 1) * parts)
        place(b, actp_ref[rows, :].astype(F32), 0)
        mean = summed[rows] / divisor[:, b : b + 1]
        place(b, mean.astype(BF).astype(F32), 1)
    out_ref[...] = tmp_ref[...].astype(BF)


def decode_kernel(
    recv_ref, self_ref, near_ref, pair_ref, wout_ref, slots_ref, label_ref,
    loss_ref, out_ref, tmp_ref, back_ref,
):
    parts = recv_ref.shape[0] // 16
    pairs = slots_ref.shape[1]
    width = self_ref.shape[0]
    tmp_ref[...] = recv_ref[...].astype(F32)

    def rows_of(kind):
        halves = [
            jnp.concatenate(
                [
                    tmp_ref[pl.ds(s * 4 + kind * 2 + c, parts, stride=16), :]
                    for s in range(4)
                ],
                1,
            )
            for c in range(2)
        ]
        return jnp.concatenate(halves, 0).astype(BF)

    embed = (
        jnp.dot(rows_of(0), self_ref[...], preferred_element_type=F32)
        + jnp.dot(rows_of(1), near_ref[...], preferred_element_type=F32)
    ).astype(BF)
    place = lax.broadcasted_iota(jnp.int32, (2 * parts, pairs), 0)
    slot = jnp.where(place < parts, 2 * place, 2 * (place - parts) + 1)
    left_pick = jnp.where(slot == slots_ref[0:1, :], 1.0, 0.0).astype(BF)
    right_pick = jnp.where(slot == slots_ref[1:2, :], 1.0, 0.0).astype(BF)
    left = contract_first(left_pick, embed)
    right = contract_first(right_pick, embed)
    product = (left * right).astype(BF)
    pre_act = (
        jnp.dot(left.astype(BF), pair_ref[0:width, :], preferred_element_type=F32)
        + jnp.dot(right.astype(BF), pair_ref[width : 2 * width, :], preferred_element_type=F32)
        + jnp.dot(product, pair_ref[2 * width : 3 * width, :], preferred_element_type=F32)
    )
    gate = jax.nn.sigmoid(pre_act)
    wout = wout_ref[...]
    logit = jnp.sum(pre_act * gate * wout, axis=1, keepdims=True)
    target = jnp.broadcast_to(label_ref[...].astype(F32), (pairs, pairs)).T[:, 0:1]
    loss = jnp.maximum(logit, 0.0) + jnp.log1p(jnp.exp(-jnp.abs(logit))) - target * logit
    loss_ref[...] = jnp.broadcast_to(loss, (pairs, pairs)).T[0:1, :]
    outer = jax.nn.sigmoid(logit) - target
    pre_grad = (outer * wout * gate * (1.0 + pre_act * (1.0 - gate))).astype(BF)
    feat = lax.dot_general(
        pre_grad, pair_ref[...], (((1,), (1,)), ((), ())), preferred_element_type=F32
    )
    third = feat[:, 2 * width :]
    left_grad = (feat[:, :width] + third * right).astype(BF)
    right_grad = (feat[:, width : 2 * width] + third * left).astype(BF)
    back = jnp.dot(left_pick, left_grad, preferred_element_type=F32) + jnp.dot(
        right_pick, right_grad, preferred_element_type=F32
    )
    for s in range(4):
        for c in range(2):
            back_ref[pl.ds(s * 2 + c, parts, stride=8), :] = back[
                c * parts : (c + 1) * parts, s * 128 : (s + 1) * 128
            ]
    out_ref[...] = back_ref[...].astype(BF)


def owner_kernel(recv_ref, push_ref, out_ref, tmp_ref):
    groups, parts = push_ref.shape
    tmp_ref[...] = recv_ref[...].astype(F32)
    grads = jnp.concatenate(
        [tmp_ref[pl.ds(b, parts, stride=groups), :] for b in range(groups)], 0
    ).astype(BF)
    firm = lax.broadcasted_iota(jnp.int32, (out_ref.shape[0], parts), 0)
    pick = jnp.concatenate(
        [
            jnp.where(firm == push_ref[b : b + 1, :], 1.0, 0.0).astype(BF)
            for b in range(groups)
        ],
        1,
    )
    out_ref[...] = jnp.dot(pick, grads, preferred_element_type=F32)


def per_device(
    firm_act, w_self, w_nbr, halo_rows, nbr_index, nbr_count, w_pair, w_out, push_rows,
    pair_slots, labels,
):
    firms, narrow = firm_act.shape
    doms, subs, cap = push_rows.shape[1:]
    slots = halo_rows.shape[2]
    both = ("dom", "sub")
    shape = jax.ShapeDtypeStruct
    vmem = pltpu.VMEM
    halo_t = jnp.transpose(halo_rows[0])
    push_t = jnp.transpose(push_rows[0], (1, 2, 0)).reshape(subs * cap, doms)
    pushed = doms * subs * cap
    halos = doms * slots

    fetch = ("hbm", "vmem")
    outgoing = call(
        halo_kernel, shape((halos, narrow), BF),
        [vmem((halos, narrow), F32), vmem((halos, firms), BF)],
        2 * halos * firms * narrow, 600_000, firm_act, halo_t, in_specs=[fetch, fetch],
    )
    incoming = lax.all_to_all(
        outgoing.reshape(doms, slots, narrow), "dom", 0, 0, tiled=True
    ).reshape(halos, narrow)
    near_counts, own_sum, push_act, push_count = call(
        count_kernel,
        (
            shape((pushed, halos), BF), shape((pushed, narrow), F32), shape((pushed, narrow), BF),
            shape((subs * cap, doms), F32),
        ),
        [vmem((pushed, firms), BF), vmem((pushed, firms), BF), vmem((pushed // 16, 512), F32)],
        10_000_000_000, 4_000_000,
        firm_act, push_t, jnp.transpose(nbr_index), nbr_count.reshape(1, firms),
        in_specs=[fetch] * 4,
    )
    message = call(
        mean_kernel, shape((2 * pushed, narrow), BF), [vmem((2 * pushed, narrow), F32)],
        2 * halos * pushed * narrow, 4_000_000,
        incoming, near_counts, own_sum, push_act, push_count,
    )
    arrived = lax.all_to_all(
        message.reshape(doms * subs, 2 * cap, narrow), both, 0, 0, tiled=True
    ).reshape(2 * pushed, narrow)
    pairs = labels.shape[0]
    pair_loss, back = call(
        decode_kernel,
        (shape((1, pairs), F32), shape((pushed, narrow), BF)),
        [vmem((2 * pushed, narrow), F32), vmem((pushed, narrow), F32)],
        5_000_000_000, 5_000_000,
        arrived, w_self, w_nbr, w_pair, w_out.reshape(1, -1), jnp.transpose(pair_slots),
        labels.reshape(1, pairs),
    )
    returned = lax.all_to_all(
        back.reshape(doms * subs, cap, narrow), both, 0, 0, tiled=True
    ).reshape(pushed, narrow)
    embed_grad = call(
        owner_kernel, shape((firms, narrow), F32), [vmem((pushed, narrow), F32)],
        2 * pushed * firms * narrow, 1_000_000, returned, push_t,
    )
    return (pair_loss.reshape(pairs), embed_grad)


def solution(mesh):
    in_specs = (
        P("dom", "sub"), P(), P(), P("dom", None, None), P("dom", None), P("dom"), P(), P(),
        P("dom", None, None, None), P(("dom", "sub"), None), P(("dom", "sub")),
    )
    out_specs = (P(("dom", "sub")), P("dom", "sub"))
    return jax.shard_map(
        per_device, mesh=mesh, in_specs=in_specs, out_specs=out_specs, check_vma=False
    )
```

```python
import jax
import jax.numpy as jnp
from jax import lax
from jax.experimental import pallas as pl
from jax.experimental.pallas import tpu as pltpu
from jax.sharding import PartitionSpec as P

BF = jnp.bfloat16
F32 = jnp.float32
DEAD = 4095
MIB = 1024 * 1024


def contract_first(a, b):
    return lax.dot_general(a, b, (((0,), (0,)), ((), ())), preferred_element_type=F32)


def call(kernel, out_shape, scratch, flops, nbytes, *args, in_specs=None, out_specs=None):
    where = {"hbm": pl.ANY, "vmem": pltpu.VMEM}
    specs = {}
    if in_specs is not None:
        args = [
            pltpu.with_memory_space_constraint(a, pltpu.HBM) if w[0] == "hbm" else a
            for a, w in zip(args, in_specs)
        ]
        specs["in_specs"] = [pl.BlockSpec(memory_space=where[w[-1]]) for w in in_specs]
    if out_specs is not None:
        specs["out_specs"] = [pl.BlockSpec(memory_space=where[w]) for w in out_specs]
        if len(out_specs) == 1:
            specs["out_specs"] = specs["out_specs"][0]
    return pl.pallas_call(
        kernel,
        out_shape=out_shape,
        scratch_shapes=scratch,
        **specs,
        compiler_params=pltpu.CompilerParams(vmem_limit_bytes=24 * MIB),
        cost_estimate=pl.CostEstimate(flops=flops, bytes_accessed=nbytes, transcendentals=0),
    )(*args)


def one_hot_rows(columns, width):
    number = lax.broadcasted_iota(jnp.int32, (columns.shape[0], width), 1)
    return [
        jnp.where(columns[:, j : j + 1] == number, 1.0, 0.0).astype(BF)
        for j in range(columns.shape[1])
    ]


def halo_kernel(act_ref, rows_ref, out_ref, tmp_ref, pick_ref):
    slots, parts = rows_ref.shape
    for j, rows in enumerate(one_hot_rows(rows_ref[...].T, act_ref.shape[0])):
        pick_ref[j * parts : (j + 1) * parts, :] = rows
    picked = jnp.dot(pick_ref[...], act_ref[...], preferred_element_type=F32)
    for j in range(slots):
        tmp_ref[pl.ds(j, parts, stride=slots), :] = picked[j * parts : (j + 1) * parts]
    out_ref[...] = tmp_ref[...].astype(BF)


def count_kernel(
    act_ref, push_ref, nbr_ref, cnt_ref, near_ref, own_ref, actp_ref, cntp_ref,
    pick_ref, mine_ref, where_ref,
):
    groups, parts = push_ref.shape
    firms = act_ref.shape[0]
    degree = nbr_ref.shape[0]
    pushed = groups * parts
    i32, i16 = jnp.int32, jnp.int16
    for j, rows in enumerate(one_hot_rows(push_ref[...].T, firms)):
        pick_ref[j * parts : (j + 1) * parts, :] = rows
    pick = pick_ref[...]
    count = cnt_ref[...]
    live = lax.broadcasted_iota(i32, (degree, firms), 0) < count
    slot = jnp.where(live, nbr_ref[...], DEAD)
    counts = jnp.broadcast_to(count, (degree, firms))
    stack = jnp.concatenate([slot >> 7, slot & 127, counts], 0).astype(F32).astype(BF)
    chosen = lax.dot_general(
        pick, stack, (((1,), (1,)), ((), ())), preferred_element_type=F32
    )
    for j in range(groups):
        block = chosen[j * parts : (j + 1) * parts, 2 * degree : 3 * degree]
        cntp_ref[j : j + 1, :] = block.T[0:1, :]
    actp_ref[...] = jnp.dot(pick, act_ref[...], preferred_element_type=F32).astype(BF)
    batch = 16
    span = batch * degree
    shape = (2 * degree, 2 * span)
    lane = lax.broadcasted_iota(i32, shape, 1)
    spread = jnp.where(
        lax.broadcasted_iota(i32, shape, 0) == (lane // span) * degree + lane % degree, 1.0, 0.0
    ).astype(BF)
    wide = jnp.dot(chosen[:, : 2 * degree].astype(BF), spread, preferred_element_type=F32)
    row = lax.broadcasted_iota(i32, (pushed, 2 * span), 0) % batch
    lane = (lax.broadcasted_iota(i32, (pushed, 2 * span), 1) % span) // degree
    wide = jnp.where(row == lane, wide, 0.0).astype(BF)
    shape = (pushed // batch, pushed)
    gather = jnp.where(
        lax.broadcasted_iota(i32, shape, 1) // batch == lax.broadcasted_iota(i32, shape, 0), 1.0, 0.0
    ).astype(BF)
    where_ref[...] = jnp.dot(gather, wide, preferred_element_type=F32)
    own_row = (
        lax.broadcasted_iota(i32, (batch, span), 1) // degree
        == lax.broadcasted_iota(i32, (batch, span), 0)
    )
    low_number = lax.broadcasted_iota(i32, (128, span), 0).astype(i16)
    one = jnp.ones((batch, span), BF)
    zero = jnp.zeros((batch, span), BF)
    mine_blocks = firms // 128
    near_blocks = near_ref.shape[1] // 128

    def fill(g, carry):
        line = where_ref[pl.ds(g, 1), :]
        high = jnp.where(own_row, jnp.broadcast_to(line[:, :span], (batch, span)), -1.0)
        high = high.astype(i32).astype(i16)
        lhs = jnp.concatenate(
            [jnp.where(high == i16(h), one, zero) for h in range(mine_blocks + near_blocks)], 0
        )
        low = jnp.broadcast_to(line[:, span:], (128, span)).astype(i32).astype(i16)
        rhs = jnp.where(low == low_number, jnp.ones((128, span), BF), jnp.zeros((128, span), BF))
        counts = lax.dot_general(
            lhs, rhs, (((1,), (1,)), ((), ())), preferred_element_type=F32
        ).astype(BF)
        rows = pl.ds(pl.multiple_of(g * batch, batch), batch)
        for h in range(mine_blocks):
            mine_ref[rows, h * 128 : (h + 1) * 128] = counts[h * batch : (h + 1) * batch]
        for h in range(near_blocks):
            at = (mine_blocks + h) * batch
            near_ref[rows, h * 128 : (h + 1) * 128] = counts[at : at + batch]
        return carry

    lax.fori_loop(0, pushed // batch, fill, 0, unroll=4)
    own_ref[...] = jnp.dot(mine_ref[...], act_ref[...], preferred_element_type=F32)


def mean_kernel(halo_ref, near_ref, own_ref, actp_ref, cntp_ref, out_ref, tmp_ref):
    groups, parts = cntp_ref.shape
    divisor = cntp_ref[...].T
    summed = own_ref[...] + jnp.dot(near_ref[...], halo_ref[...], preferred_element_type=F32)

    def place(b, rows, kind):
        tmp_ref[pl.ds((b // 2) * 4 + kind * 2 + b % 2, parts, stride=2 * groups), :] = rows

    for b in range(groups):
        rows = slice(b * parts, (b + 1) * parts)
        place(b, actp_ref[rows, :].astype(F32), 0)
        mean = summed[rows] / divisor[:, b : b + 1]
        place(b, mean.astype(BF).astype(F32), 1)
    out_ref[...] = tmp_ref[...].astype(BF)


def decode_kernel(
    recv_ref, self_ref, near_ref, pair_ref, wout_ref, slots_ref, label_ref,
    loss_ref, out_ref, tmp_ref, back_ref,
):
    parts = recv_ref.shape[0] // 16
    pairs = slots_ref.shape[1]
    width = self_ref.shape[0]
    tmp_ref[...] = recv_ref[...].astype(F32)

    def rows_of(kind):
        halves = [
            jnp.concatenate(
                [
                    tmp_ref[pl.ds(s * 4 + kind * 2 + c, parts, stride=16), :]
                    for s in range(4)
                ],
                1,
            )
            for c in range(2)
        ]
        return jnp.concatenate(halves, 0).astype(BF)

    embed = (
        jnp.dot(rows_of(0), self_ref[...], preferred_element_type=F32)
        + jnp.dot(rows_of(1), near_ref[...], preferred_element_type=F32)
    ).astype(BF)
    place = lax.broadcasted_iota(jnp.int32, (2 * parts, pairs), 0)
    slot = jnp.where(place < parts, 2 * place, 2 * (place - parts) + 1)
    left_pick = jnp.where(slot == slots_ref[0:1, :], 1.0, 0.0).astype(BF)
    right_pick = jnp.where(slot == slots_ref[1:2, :], 1.0, 0.0).astype(BF)
    picks = jnp.concatenate([left_pick, right_pick], 1)
    ends = contract_first(picks, embed)
    left, right = ends[:pairs], ends[pairs:]
    product = (left * right).astype(BF)
    pre_act = (
        jnp.dot(left.astype(BF), pair_ref[0:width, :], preferred_element_type=F32)
        + jnp.dot(right.astype(BF), pair_ref[width : 2 * width, :], preferred_element_type=F32)
        + jnp.dot(product, pair_ref[2 * width : 3 * width, :], preferred_element_type=F32)
    )
    gate = jax.nn.sigmoid(pre_act)
    active = pre_act * gate
    wout = wout_ref[...]
    logit = jnp.sum(active * wout, axis=1, keepdims=True)
    target = jnp.broadcast_to(label_ref[...].astype(F32), (pairs, pairs)).T[:, 0:1]
    loss = jnp.maximum(logit, 0.0) + jnp.log1p(jnp.exp(-jnp.abs(logit))) - target * logit
    loss_ref[...] = jnp.broadcast_to(loss, (pairs, pairs)).T[0:1, :]
    outer = jax.nn.sigmoid(logit) - target
    pre_grad = (wout * (gate + active * (1.0 - gate))).astype(BF)
    feat = [
        lax.dot_general(
            pre_grad, pair_ref[i * width : (i + 1) * width, :], (((1,), (1,)), ((), ())),
            preferred_element_type=F32,
        )
        for i in (2, 0, 1)
    ]
    third = outer * feat[0]
    left_grad = (outer * feat[1] + third * right).astype(BF)
    right_grad = (outer * feat[2] + third * left).astype(BF)
    back = jnp.dot(
        picks, jnp.concatenate([left_grad, right_grad], 0), preferred_element_type=F32
    )
    for s in range(4):
        for c in range(2):
            back_ref[pl.ds(s * 2 + c, parts, stride=8), :] = back[
                c * parts : (c + 1) * parts, s * 128 : (s + 1) * 128
            ]
    out_ref[...] = back_ref[...].astype(BF)


def owner_kernel(recv_ref, push_ref, out_ref, tmp_ref, sum_ref, sems):
    groups, parts = push_ref.shape
    tmp_ref[...] = recv_ref[...].astype(F32)
    grads = jnp.concatenate(
        [tmp_ref[pl.ds(b, parts, stride=groups), :] for b in range(groups)], 0
    ).astype(BF)
    parcels = sems.shape[0]
    step = sum_ref.shape[0] // parcels
    firm = lax.broadcasted_iota(jnp.int32, (step, parts), 0)
    copies = []
    for p in range(parcels):
        pick = jnp.concatenate(
            [
                jnp.where(firm + p * step == push_ref[b : b + 1, :], 1.0, 0.0).astype(BF)
                for b in range(groups)
            ],
            1,
        )
        rows = pl.ds(p * step, step)
        sum_ref[rows, :] = jnp.dot(pick, grads, preferred_element_type=F32)
        copies.append(pltpu.make_async_copy(sum_ref.at[rows, :], out_ref.at[rows, :], sems.at[p]))
        copies[-1].start()
    for copy in copies:
        copy.wait()


def per_device(
    firm_act, w_self, w_nbr, halo_rows, nbr_index, nbr_count, w_pair, w_out, push_rows,
    pair_slots, labels,
):
    firms, narrow = firm_act.shape
    doms, subs, cap = push_rows.shape[1:]
    slots = halo_rows.shape[2]
    both = ("dom", "sub")
    shape = jax.ShapeDtypeStruct
    vmem = pltpu.VMEM
    halo_t = jnp.transpose(halo_rows[0])
    push_t = jnp.transpose(push_rows[0], (1, 2, 0)).reshape(subs * cap, doms)
    pushed = doms * subs * cap
    halos = doms * slots

    fetch = ("hbm", "vmem")
    outgoing = call(
        halo_kernel, shape((halos, narrow), BF),
        [vmem((halos, narrow), F32), vmem((halos, firms), BF)],
        2 * halos * firms * narrow, 600_000, firm_act, halo_t, in_specs=[fetch, fetch],
    )
    incoming = lax.all_to_all(
        outgoing.reshape(doms, slots, narrow), "dom", 0, 0, tiled=True
    ).reshape(halos, narrow)
    near_counts, own_sum, push_act, push_count = call(
        count_kernel,
        (
            shape((pushed, halos), BF), shape((pushed, narrow), F32), shape((pushed, narrow), BF),
            shape((subs * cap, doms), F32),
        ),
        [vmem((pushed, firms), BF), vmem((pushed, firms), BF), vmem((pushed // 16, 512), F32)],
        10_000_000_000, 4_000_000,
        firm_act, push_t, jnp.transpose(nbr_index), nbr_count.reshape(1, firms),
        in_specs=[fetch] * 4,
    )
    message = call(
        mean_kernel, shape((2 * pushed, narrow), BF), [vmem((2 * pushed, narrow), F32)],
        2 * halos * pushed * narrow, 4_000_000,
        incoming, near_counts, own_sum, push_act, push_count,
    )
    arrived = lax.all_to_all(
        message.reshape(doms * subs, 2 * cap, narrow), both, 0, 0, tiled=True
    ).reshape(2 * pushed, narrow)
    pairs = labels.shape[0]
    pair_loss, back = call(
        decode_kernel,
        (shape((1, pairs), F32), shape((pushed, narrow), BF)),
        [vmem((2 * pushed, narrow), F32), vmem((pushed, narrow), F32)],
        5_000_000_000, 5_000_000,
        arrived, w_self, w_nbr, w_pair, w_out.reshape(1, -1), jnp.transpose(pair_slots),
        labels.reshape(1, pairs),
    )
    returned = lax.all_to_all(
        back.reshape(doms * subs, cap, narrow), both, 0, 0, tiled=True
    ).reshape(pushed, narrow)
    embed_grad = call(
        owner_kernel, pltpu.HBM((firms, narrow), F32),
        [vmem((pushed, narrow), F32), vmem((firms, narrow), F32), pltpu.SemaphoreType.DMA((4,))],
        2 * pushed * firms * narrow, 1_000_000, returned, push_t,
        in_specs=[("vmem",)] * 2, out_specs=["hbm"],
    )
    return (pair_loss.reshape(pairs), embed_grad)


def solution(mesh):
    in_specs = (
        P("dom", "sub"), P(), P(), P("dom", None, None), P("dom", None), P("dom"), P(), P(),
        P("dom", None, None, None), P(("dom", "sub"), None), P(("dom", "sub")),
    )
    out_specs = (P(("dom", "sub")), P("dom", "sub"))
    return jax.shard_map(
        per_device, mesh=mesh, in_specs=in_specs, out_specs=out_specs, check_vma=False
    )
```

```python
import jax
import jax.numpy as jnp
from jax import lax
from jax.experimental import pallas as pl
from jax.experimental.pallas import tpu as pltpu
from jax.sharding import PartitionSpec as P

BF = jnp.bfloat16
F32 = jnp.float32
CORES = 2
YS = 8
DEAD = 4095
MIB = 1024 * 1024


def contract_first(a, b):
    return lax.dot_general(a, b, (((0,), (0,)), ((), ())), preferred_element_type=F32)


def call(kernel, out_shape, scratch, flops, nbytes, *args, in_specs=None, out_specs=None):
    where = {"hbm": pl.ANY, "vmem": pltpu.VMEM}
    specs = {}
    if in_specs is not None:
        args = [
            pltpu.with_memory_space_constraint(a, pltpu.HBM) if w[0] == "hbm" else a
            for a, w in zip(args, in_specs)
        ]
        specs["in_specs"] = [pl.BlockSpec(memory_space=where[w[-1]]) for w in in_specs]
    if out_specs is not None:
        specs["out_specs"] = [pl.BlockSpec(memory_space=where[w]) for w in out_specs]
        if len(out_specs) == 1:
            specs["out_specs"] = specs["out_specs"][0]
    return pl.pallas_call(
        kernel,
        out_shape=out_shape,
        scratch_shapes=scratch,
        **specs,
        compiler_params=pltpu.CompilerParams(vmem_limit_bytes=24 * MIB),
        cost_estimate=pl.CostEstimate(flops=flops, bytes_accessed=nbytes, transcendentals=0),
    )(*args)


def one_hot_rows(columns, width):
    number = lax.broadcasted_iota(jnp.int32, (columns.shape[0], width), 1)
    return [
        jnp.where(columns[:, j : j + 1] == number, 1.0, 0.0).astype(BF)
        for j in range(columns.shape[1])
    ]


def halo_kernel(act_ref, rows_ref, out_ref, tmp_ref, pick_ref):
    slots, parts = rows_ref.shape
    for j, rows in enumerate(one_hot_rows(rows_ref[...].T, act_ref.shape[0])):
        pick_ref[j * parts : (j + 1) * parts, :] = rows
    picked = jnp.dot(pick_ref[...], act_ref[...], preferred_element_type=F32)
    for j in range(slots):
        tmp_ref[pl.ds(j, parts, stride=slots), :] = picked[j * parts : (j + 1) * parts]
    out_ref[...] = tmp_ref[...].astype(BF)


def count_kernel(
    act_ref, push_ref, nbr_ref, cnt_ref, near_ref, own_ref, actp_ref, cntp_ref, order_ref,
    pick_ref, mine_ref, where_ref, turn_ref,
):
    groups, parts = push_ref.shape
    firms = act_ref.shape[0]
    degree = nbr_ref.shape[0]
    pushed = groups * parts
    i32, i16 = jnp.int32, jnp.int16
    turn_ref[...] = push_ref[...].T
    order = jnp.concatenate(
        [
            turn_ref[pl.ds(z * CORES + c, YS, stride=parts // YS), :]
            for c in range(CORES)
            for z in range(parts // YS // CORES)
        ],
        0,
    )
    order_ref[...] = order.T
    for j, rows in enumerate(one_hot_rows(order, firms)):
        pick_ref[j * parts : (j + 1) * parts, :] = rows
    pick = pick_ref[...]
    count = cnt_ref[...]
    live = lax.broadcasted_iota(i32, (degree, firms), 0) < count
    slot = jnp.where(live, nbr_ref[...], DEAD)
    counts = jnp.broadcast_to(count, (degree, firms))
    stack = jnp.concatenate([slot >> 7, slot & 127, counts], 0).astype(F32).astype(BF)
    chosen = lax.dot_general(
        pick, stack, (((1,), (1,)), ((), ())), preferred_element_type=F32
    )
    for j in range(groups):
        block = chosen[j * parts : (j + 1) * parts, 2 * degree : 3 * degree]
        cntp_ref[j : j + 1, :] = block.T[0:1, :]
    actp_ref[...] = jnp.dot(pick, act_ref[...], preferred_element_type=F32).astype(BF)
    batch = 16
    span = batch * degree
    shape = (2 * degree, 2 * span)
    lane = lax.broadcasted_iota(i32, shape, 1)
    spread = jnp.where(
        lax.broadcasted_iota(i32, shape, 0) == (lane // span) * degree + lane % degree, 1.0, 0.0
    ).astype(BF)
    wide = jnp.dot(chosen[:, : 2 * degree].astype(BF), spread, preferred_element_type=F32)
    row = lax.broadcasted_iota(i32, (pushed, 2 * span), 0) % batch
    lane = (lax.broadcasted_iota(i32, (pushed, 2 * span), 1) % span) // degree
    wide = jnp.where(row == lane, wide, 0.0).astype(BF)
    shape = (pushed // batch, pushed)
    gather = jnp.where(
        lax.broadcasted_iota(i32, shape, 1) // batch == lax.broadcasted_iota(i32, shape, 0), 1.0, 0.0
    ).astype(BF)
    where_ref[...] = jnp.dot(gather, wide, preferred_element_type=F32)
    own_row = (
        lax.broadcasted_iota(i32, (batch, span), 1) // degree
        == lax.broadcasted_iota(i32, (batch, span), 0)
    )
    low_number = lax.broadcasted_iota(i32, (128, span), 0).astype(i16)
    one = jnp.ones((batch, span), BF)
    zero = jnp.zeros((batch, span), BF)
    mine_blocks = firms // 128
    near_blocks = near_ref.shape[1] // 128

    def fill(g, carry):
        line = where_ref[pl.ds(g, 1), :]
        high = jnp.where(own_row, jnp.broadcast_to(line[:, :span], (batch, span)), -1.0)
        high = high.astype(i32).astype(i16)
        lhs = jnp.concatenate(
            [jnp.where(high == i16(h), one, zero) for h in range(mine_blocks + near_blocks)], 0
        )
        low = jnp.broadcast_to(line[:, span:], (128, span)).astype(i32).astype(i16)
        rhs = jnp.where(low == low_number, jnp.ones((128, span), BF), jnp.zeros((128, span), BF))
        counts = lax.dot_general(
            lhs, rhs, (((1,), (1,)), ((), ())), preferred_element_type=F32
        ).astype(BF)
        rows = pl.ds(pl.multiple_of(g * batch, batch), batch)
        for h in range(mine_blocks):
            mine_ref[rows, h * 128 : (h + 1) * 128] = counts[h * batch : (h + 1) * batch]
        for h in range(near_blocks):
            at = (mine_blocks + h) * batch
            near_ref[rows, h * 128 : (h + 1) * 128] = counts[at : at + batch]
        return carry

    lax.fori_loop(0, pushed // batch, fill, 0, unroll=4)
    own_ref[...] = jnp.dot(mine_ref[...], act_ref[...], preferred_element_type=F32)


def mean_kernel(halo_ref, near_ref, own_ref, actp_ref, cntp_ref, out_ref, tmp_ref):
    groups, parts = cntp_ref.shape
    divisor = cntp_ref[...].T
    summed = own_ref[...] + jnp.dot(near_ref[...], halo_ref[...], preferred_element_type=F32)

    half = parts // CORES

    def place(b, rows, kind):
        for c in range(CORES):
            at = (c * groups // 2 + b // 2) * half * 4 + kind * 2 + b % 2
            tmp_ref[pl.ds(at, half, stride=4), :] = rows[c * half : (c + 1) * half]

    for b in range(groups):
        rows = slice(b * parts, (b + 1) * parts)
        place(b, actp_ref[rows, :].astype(F32), 0)
        mean = summed[rows] / divisor[:, b : b + 1]
        place(b, mean.astype(BF).astype(F32), 1)
    out_ref[...] = tmp_ref[...].astype(BF)


def decode_kernel(
    recv_ref, self_ref, near_ref, pair_ref, wout_ref, slots_ref, label_ref,
    loss_ref, out_ref, tmp_ref, back_ref,
):
    parts = recv_ref.shape[0] // 16
    pairs = slots_ref.shape[1]
    width = self_ref.shape[0]
    tmp_ref[...] = recv_ref[...].astype(F32)

    half = parts // CORES

    def rows_of(kind):
        return jnp.concatenate(
            [
                jnp.concatenate(
                    [
                        tmp_ref[pl.ds((c * 4 + s) * half * 4 + kind * 2 + cap, half, stride=4), :]
                        for s in range(4)
                    ],
                    1,
                )
                for cap in range(2)
                for c in range(CORES)
            ],
            0,
        ).astype(BF)

    embed = (
        jnp.dot(rows_of(0), self_ref[...], preferred_element_type=F32)
        + jnp.dot(rows_of(1), near_ref[...], preferred_element_type=F32)
    ).astype(BF)
    place = lax.broadcasted_iota(jnp.int32, (2 * parts, pairs), 0)
    y, z, c = place % YS, place % half // YS, place % parts // half
    slot = ((y * (half // YS) + z) * CORES + c) * 2 + place // parts
    left_pick = jnp.where(slot == slots_ref[0:1, :], 1.0, 0.0).astype(BF)
    right_pick = jnp.where(slot == slots_ref[1:2, :], 1.0, 0.0).astype(BF)
    picks = jnp.concatenate([left_pick, right_pick], 1)
    ends = contract_first(picks, embed)
    left, right = ends[:pairs], ends[pairs:]
    product = (left * right).astype(BF)
    pre_act = (
        jnp.dot(left.astype(BF), pair_ref[0:width, :], preferred_element_type=F32)
        + jnp.dot(right.astype(BF), pair_ref[width : 2 * width, :], preferred_element_type=F32)
        + jnp.dot(product, pair_ref[2 * width : 3 * width, :], preferred_element_type=F32)
    )
    gate = jax.nn.sigmoid(pre_act)
    active = pre_act * gate
    wout = wout_ref[...]
    logit = jnp.sum(active * wout, axis=1, keepdims=True)
    target = jnp.broadcast_to(label_ref[...].astype(F32), (pairs, pairs)).T[:, 0:1]
    loss = jnp.maximum(logit, 0.0) + jnp.log1p(jnp.exp(-jnp.abs(logit))) - target * logit
    loss_ref[...] = jnp.broadcast_to(loss, (pairs, pairs)).T[0:1, :]
    outer = jax.nn.sigmoid(logit) - target
    pre_grad = (wout * (gate + active * (1.0 - gate))).astype(BF)
    feat = [
        lax.dot_general(
            pre_grad, pair_ref[i * width : (i + 1) * width, :], (((1,), (1,)), ((), ())),
            preferred_element_type=F32,
        )
        for i in (2, 0, 1)
    ]
    third = outer * feat[0]
    left_grad = (outer * feat[1] + third * right).astype(BF)
    right_grad = (outer * feat[2] + third * left).astype(BF)
    back = jnp.dot(
        picks, jnp.concatenate([left_grad, right_grad], 0), preferred_element_type=F32
    )
    for s in range(4):
        for cap in range(2):
            for c in range(CORES):
                at = cap * parts + c * half
                back_ref[pl.ds((c * 4 + s) * half * 2 + cap, half, stride=2), :] = back[
                    at : at + half, s * 128 : (s + 1) * 128
                ]
    out_ref[...] = back_ref[...].astype(BF)


def owner_kernel(recv_ref, push_ref, out_ref, tmp_ref, sum_ref, sems):
    groups, parts = push_ref.shape
    tmp_ref[...] = recv_ref[...].astype(F32)
    half = parts // CORES
    grads = jnp.concatenate(
        [
            tmp_ref[pl.ds((c * groups // 2 + b // 2) * half * 2 + b % 2, half, stride=2), :]
            for b in range(groups)
            for c in range(CORES)
        ],
        0,
    ).astype(BF)
    parcels = sems.shape[0]
    step = sum_ref.shape[0] // parcels
    firm = lax.broadcasted_iota(jnp.int32, (step, parts), 0)
    copies = []
    for p in range(parcels):
        pick = jnp.concatenate(
            [
                jnp.where(firm + p * step == push_ref[b : b + 1, :], 1.0, 0.0).astype(BF)
                for b in range(groups)
            ],
            1,
        )
        rows = pl.ds(p * step, step)
        sum_ref[rows, :] = jnp.dot(pick, grads, preferred_element_type=F32)
        copies.append(pltpu.make_async_copy(sum_ref.at[rows, :], out_ref.at[rows, :], sems.at[p]))
        copies[-1].start()
    for copy in copies:
        copy.wait()


def per_device(
    firm_act, w_self, w_nbr, halo_rows, nbr_index, nbr_count, w_pair, w_out, push_rows,
    pair_slots, labels,
):
    firms, narrow = firm_act.shape
    doms, subs, cap = push_rows.shape[1:]
    slots = halo_rows.shape[2]
    dom, everyone = ("y", "z", "c"), ("c", "x", "z", "y")
    shape = jax.ShapeDtypeStruct
    vmem = pltpu.VMEM
    halo_t = jnp.transpose(halo_rows[0])
    push_t = jnp.transpose(push_rows[0], (1, 2, 0)).reshape(subs * cap, doms)
    pushed = doms * subs * cap
    halos = doms * slots

    fetch = ("hbm", "vmem")
    outgoing = call(
        halo_kernel, shape((halos, narrow), BF),
        [vmem((halos, narrow), F32), vmem((halos, firms), BF)],
        2 * halos * firms * narrow, 600_000, firm_act, halo_t, in_specs=[fetch, fetch],
    )
    incoming = lax.all_to_all(
        outgoing.reshape(doms, slots, narrow), dom, 0, 0, tiled=True
    ).reshape(halos, narrow)
    near_counts, own_sum, push_act, push_count, push_order = call(
        count_kernel,
        (
            shape((pushed, halos), BF), shape((pushed, narrow), F32), shape((pushed, narrow), BF),
            shape((subs * cap, doms), F32), shape((subs * cap, doms), jnp.int32),
        ),
        [
            vmem((pushed, firms), BF), vmem((pushed, firms), BF), vmem((pushed // 16, 512), F32),
            vmem((doms, subs * cap), jnp.int32),
        ],
        10_000_000_000, 4_000_000,
        firm_act, push_t, jnp.transpose(nbr_index), nbr_count.reshape(1, firms),
        in_specs=[fetch] * 4,
    )
    message = call(
        mean_kernel, shape((2 * pushed, narrow), BF), [vmem((2 * pushed, narrow), F32)],
        2 * halos * pushed * narrow, 4_000_000,
        incoming, near_counts, own_sum, push_act, push_count,
    )
    arrived = lax.all_to_all(
        message.reshape(doms * subs, 2 * cap, narrow), everyone, 0, 0, tiled=True
    ).reshape(2 * pushed, narrow)
    pairs = labels.shape[0]
    pair_loss, back = call(
        decode_kernel,
        (shape((1, pairs), F32), shape((pushed, narrow), BF)),
        [vmem((2 * pushed, narrow), F32), vmem((pushed, narrow), F32)],
        5_000_000_000, 5_000_000,
        arrived, w_self, w_nbr, w_pair, w_out.reshape(1, -1), jnp.transpose(pair_slots),
        labels.reshape(1, pairs),
    )
    returned = lax.all_to_all(
        back.reshape(doms * subs, cap, narrow), everyone, 0, 0, tiled=True
    ).reshape(pushed, narrow)
    embed_grad = call(
        owner_kernel, pltpu.HBM((firms, narrow), F32),
        [vmem((pushed, narrow), F32), vmem((firms, narrow), F32), pltpu.SemaphoreType.DMA((4,))],
        2 * pushed * firms * narrow, 1_000_000, returned, push_order,
        in_specs=[("vmem",)] * 2, out_specs=["hbm"],
    )
    return (pair_loss.reshape(pairs), embed_grad)


def solution(mesh):
    subs = mesh.shape["sub"]
    zs = mesh.shape["dom"] // YS // CORES
    cut = jax.sharding.Mesh(mesh.devices.reshape(YS, zs, CORES, subs), ("y", "z", "c", "x"))
    dom, every = ("y", "z", "c"), ("y", "z", "c", "x")
    in_specs = (
        P(dom, "x"), P(), P(), P(dom, None, None), P(dom, None), P(dom), P(), P(),
        P(dom, None, None, None), P(every, None), P(every),
    )
    out_specs = (P(every), P(dom, "x"))
    return jax.shard_map(
        per_device, mesh=cut, in_specs=in_specs, out_specs=out_specs, check_vma=False
    )
```

```python
import jax
import jax.numpy as jnp
from jax import lax
from jax.experimental import pallas as pl
from jax.experimental.pallas import tpu as pltpu
from jax.sharding import PartitionSpec as P

BF = jnp.bfloat16
F32 = jnp.float32
DEAD = 4095
MIB = 1024 * 1024


def contract_first(a, b):
    return lax.dot_general(a, b, (((0,), (0,)), ((), ())), preferred_element_type=F32)


def call(kernel, out_shape, scratch, flops, nbytes, *args, in_specs=None, out_specs=None):
    where = {"hbm": pl.ANY, "vmem": pltpu.VMEM}
    specs = {}
    if in_specs is not None:
        args = [
            pltpu.with_memory_space_constraint(a, pltpu.HBM) if w[0] == "hbm" else a
            for a, w in zip(args, in_specs)
        ]
        specs["in_specs"] = [pl.BlockSpec(memory_space=where[w[-1]]) for w in in_specs]
    if out_specs is not None:
        specs["out_specs"] = [pl.BlockSpec(memory_space=where[w]) for w in out_specs]
        if len(out_specs) == 1:
            specs["out_specs"] = specs["out_specs"][0]
    return pl.pallas_call(
        kernel,
        out_shape=out_shape,
        scratch_shapes=scratch,
        **specs,
        compiler_params=pltpu.CompilerParams(vmem_limit_bytes=24 * MIB),
        cost_estimate=pl.CostEstimate(flops=flops, bytes_accessed=nbytes, transcendentals=0),
    )(*args)


def one_hot_rows(columns, width):
    number = lax.broadcasted_iota(jnp.int32, (columns.shape[0], width), 1)
    return [
        jnp.where(columns[:, j : j + 1] == number, 1.0, 0.0).astype(BF)
        for j in range(columns.shape[1])
    ]


def halo_kernel(act_ref, rows_ref, out_ref, tmp_ref, pick_ref):
    slots, parts = rows_ref.shape
    for j, rows in enumerate(one_hot_rows(rows_ref[...].T, act_ref.shape[0])):
        pick_ref[j * parts : (j + 1) * parts, :] = rows
    picked = jnp.dot(pick_ref[...], act_ref[...], preferred_element_type=F32)
    for j in range(slots):
        tmp_ref[pl.ds(j, parts, stride=slots), :] = picked[j * parts : (j + 1) * parts]
    out_ref[...] = tmp_ref[...].astype(BF)


def count_kernel(
    act_ref, push_ref, nbr_ref, cnt_ref, near_ref, own_ref, actp_ref, cntp_ref,
    pick_ref, mine_ref, where_ref,
):
    groups, parts = push_ref.shape
    firms = act_ref.shape[0]
    degree = nbr_ref.shape[0]
    pushed = groups * parts
    i32, i16 = jnp.int32, jnp.int16
    for j, rows in enumerate(one_hot_rows(push_ref[...].T, firms)):
        pick_ref[j * parts : (j + 1) * parts, :] = rows
    pick = pick_ref[...]
    count = cnt_ref[...]
    live = lax.broadcasted_iota(i32, (degree, firms), 0) < count
    slot = jnp.where(live, nbr_ref[...], DEAD)
    counts = jnp.broadcast_to(count, (degree, firms))
    stack = jnp.concatenate([slot >> 7, slot & 127, counts], 0).astype(F32).astype(BF)
    chosen = lax.dot_general(
        pick, stack, (((1,), (1,)), ((), ())), preferred_element_type=F32
    )
    for j in range(groups):
        block = chosen[j * parts : (j + 1) * parts, 2 * degree : 3 * degree]
        cntp_ref[j : j + 1, :] = block.T[0:1, :]
    actp_ref[...] = jnp.dot(pick, act_ref[...], preferred_element_type=F32).astype(BF)
    batch = 16
    span = batch * degree
    shape = (2 * degree, 2 * span)
    lane = lax.broadcasted_iota(i32, shape, 1)
    spread = jnp.where(
        lax.broadcasted_iota(i32, shape, 0) == (lane // span) * degree + lane % degree, 1.0, 0.0
    ).astype(BF)
    wide = jnp.dot(chosen[:, : 2 * degree].astype(BF), spread, preferred_element_type=F32)
    row = lax.broadcasted_iota(i32, (pushed, 2 * span), 0) % batch
    lane = (lax.broadcasted_iota(i32, (pushed, 2 * span), 1) % span) // degree
    wide = jnp.where(row == lane, wide, 0.0).astype(BF)
    shape = (pushed // batch, pushed)
    gather = jnp.where(
        lax.broadcasted_iota(i32, shape, 1) // batch == lax.broadcasted_iota(i32, shape, 0), 1.0, 0.0
    ).astype(BF)
    where_ref[...] = jnp.dot(gather, wide, preferred_element_type=F32)
    own_row = (
        lax.broadcasted_iota(i32, (batch, span), 1) // degree
        == lax.broadcasted_iota(i32, (batch, span), 0)
    )
    low_number = lax.broadcasted_iota(i32, (128, span), 0).astype(i16)
    one = jnp.ones((batch, span), BF)
    zero = jnp.zeros((batch, span), BF)
    mine_blocks = firms // 128
    near_blocks = near_ref.shape[1] // 128

    def fill(g, carry):
        line = where_ref[pl.ds(g, 1), :]
        high = jnp.where(own_row, jnp.broadcast_to(line[:, :span], (batch, span)), -1.0)
        high = high.astype(i32).astype(i16)
        lhs = jnp.concatenate(
            [jnp.where(high == i16(h), one, zero) for h in range(mine_blocks + near_blocks)], 0
        )
        low = jnp.broadcast_to(line[:, span:], (128, span)).astype(i32).astype(i16)
        rhs = jnp.where(low == low_number, jnp.ones((128, span), BF), jnp.zeros((128, span), BF))
        counts = lax.dot_general(
            lhs, rhs, (((1,), (1,)), ((), ())), preferred_element_type=F32
        ).astype(BF)
        rows = pl.ds(pl.multiple_of(g * batch, batch), batch)
        for h in range(mine_blocks):
            mine_ref[rows, h * 128 : (h + 1) * 128] = counts[h * batch : (h + 1) * batch]
        for h in range(near_blocks):
            at = (mine_blocks + h) * batch
            near_ref[rows, h * 128 : (h + 1) * 128] = counts[at : at + batch]
        return carry

    lax.fori_loop(0, pushed // batch, fill, 0, unroll=4)
    own_ref[...] = jnp.dot(mine_ref[...], act_ref[...], preferred_element_type=F32)


def mean_kernel(halo_ref, near_ref, own_ref, actp_ref, cntp_ref, out_ref, tmp_ref):
    groups, parts = cntp_ref.shape
    divisor = cntp_ref[...].T
    summed = own_ref[...] + jnp.dot(near_ref[...], halo_ref[...], preferred_element_type=F32)

    def place(b, rows, kind):
        tmp_ref[pl.ds((b // 2) * parts * 4 + kind * 2 + b % 2, parts, stride=4), :] = rows

    for b in range(groups):
        rows = slice(b * parts, (b + 1) * parts)
        place(b, actp_ref[rows, :].astype(F32), 0)
        mean = summed[rows] / divisor[:, b : b + 1]
        place(b, mean.astype(BF).astype(F32), 1)
    out_ref[...] = tmp_ref[...].astype(BF)


def decode_kernel(
    recv_ref, self_ref, near_ref, pair_ref, wout_ref, slots_ref, label_ref,
    loss_ref, out_ref, tmp_ref, back_ref,
):
    parts = recv_ref.shape[0] // 16
    pairs = slots_ref.shape[1]
    width = self_ref.shape[0]
    tmp_ref[...] = recv_ref[...].astype(F32)

    def rows_of(kind):
        halves = [
            jnp.concatenate(
                [
                    tmp_ref[pl.ds(s * parts * 4 + kind * 2 + c, parts, stride=4), :]
                    for s in range(4)
                ],
                1,
            )
            for c in range(2)
        ]
        return jnp.concatenate(halves, 0).astype(BF)

    embed = (
        jnp.dot(rows_of(0), self_ref[...], preferred_element_type=F32)
        + jnp.dot(rows_of(1), near_ref[...], preferred_element_type=F32)
    ).astype(BF)
    place = lax.broadcasted_iota(jnp.int32, (2 * parts, pairs), 0)
    slot = jnp.where(place < parts, 2 * place, 2 * (place - parts) + 1)
    left_pick = jnp.where(slot == slots_ref[0:1, :], 1.0, 0.0).astype(BF)
    right_pick = jnp.where(slot == slots_ref[1:2, :], 1.0, 0.0).astype(BF)
    picks = jnp.concatenate([left_pick, right_pick], 1)
    ends = contract_first(picks, embed)
    left, right = ends[:pairs], ends[pairs:]
    product = (left * right).astype(BF)
    pre_act = (
        jnp.dot(left.astype(BF), pair_ref[0:width, :], preferred_element_type=F32)
        + jnp.dot(right.astype(BF), pair_ref[width : 2 * width, :], preferred_element_type=F32)
        + jnp.dot(product, pair_ref[2 * width : 3 * width, :], preferred_element_type=F32)
    )
    gate = jax.nn.sigmoid(pre_act)
    active = pre_act * gate
    wout = wout_ref[...]
    logit = jnp.sum(active * wout, axis=1, keepdims=True)
    target = jnp.broadcast_to(label_ref[...].astype(F32), (pairs, pairs)).T[:, 0:1]
    loss = jnp.maximum(logit, 0.0) + jnp.log1p(jnp.exp(-jnp.abs(logit))) - target * logit
    loss_ref[...] = jnp.broadcast_to(loss, (pairs, pairs)).T[0:1, :]
    outer = jax.nn.sigmoid(logit) - target
    pre_grad = (wout * (gate + active * (1.0 - gate))).astype(BF)
    feat = [
        lax.dot_general(
            pre_grad, pair_ref[i * width : (i + 1) * width, :], (((1,), (1,)), ((), ())),
            preferred_element_type=F32,
        )
        for i in (2, 0, 1)
    ]
    third = outer * feat[0]
    left_grad = (outer * feat[1] + third * right).astype(BF)
    right_grad = (outer * feat[2] + third * left).astype(BF)
    back = jnp.dot(
        picks, jnp.concatenate([left_grad, right_grad], 0), preferred_element_type=F32
    )
    for s in range(4):
        for c in range(2):
            back_ref[pl.ds(s * parts * 2 + c, parts, stride=2), :] = back[
                c * parts : (c + 1) * parts, s * 128 : (s + 1) * 128
            ]
    out_ref[...] = back_ref[...].astype(BF)


def owner_kernel(recv_ref, push_ref, out_ref, tmp_ref, sum_ref, sems):
    groups, parts = push_ref.shape
    tmp_ref[...] = recv_ref[...].astype(F32)
    grads = jnp.concatenate(
        [tmp_ref[pl.ds((b // 2) * parts * 2 + b % 2, parts, stride=2), :]
            for b in range(groups)], 0
    ).astype(BF)
    parcels = sems.shape[0]
    step = sum_ref.shape[0] // parcels
    firm = lax.broadcasted_iota(jnp.int32, (step, parts), 0)
    copies = []
    for p in range(parcels):
        pick = jnp.concatenate(
            [
                jnp.where(firm + p * step == push_ref[b : b + 1, :], 1.0, 0.0).astype(BF)
                for b in range(groups)
            ],
            1,
        )
        rows = pl.ds(p * step, step)
        sum_ref[rows, :] = jnp.dot(pick, grads, preferred_element_type=F32)
        copies.append(pltpu.make_async_copy(sum_ref.at[rows, :], out_ref.at[rows, :], sems.at[p]))
        copies[-1].start()
    for copy in copies:
        copy.wait()


def per_device(
    firm_act, w_self, w_nbr, halo_rows, nbr_index, nbr_count, w_pair, w_out, push_rows,
    pair_slots, labels,
):
    firms, narrow = firm_act.shape
    doms, subs, cap = push_rows.shape[1:]
    slots = halo_rows.shape[2]
    both = ("sub", "dom")
    shape = jax.ShapeDtypeStruct
    vmem = pltpu.VMEM
    halo_t = jnp.transpose(halo_rows[0])
    push_t = jnp.transpose(push_rows[0], (1, 2, 0)).reshape(subs * cap, doms)
    pushed = doms * subs * cap
    halos = doms * slots

    fetch = ("hbm", "vmem")
    outgoing = call(
        halo_kernel, shape((halos, narrow), BF),
        [vmem((halos, narrow), F32), vmem((halos, firms), BF)],
        2 * halos * firms * narrow, 600_000, firm_act, halo_t, in_specs=[fetch, fetch],
    )
    incoming = lax.all_to_all(
        outgoing.reshape(doms, slots, narrow), "dom", 0, 0, tiled=True
    ).reshape(halos, narrow)
    near_counts, own_sum, push_act, push_count = call(
        count_kernel,
        (
            shape((pushed, halos), BF), shape((pushed, narrow), F32), shape((pushed, narrow), BF),
            shape((subs * cap, doms), F32),
        ),
        [vmem((pushed, firms), BF), vmem((pushed, firms), BF), vmem((pushed // 16, 512), F32)],
        10_000_000_000, 4_000_000,
        firm_act, push_t, jnp.transpose(nbr_index), nbr_count.reshape(1, firms),
        in_specs=[fetch] * 4,
    )
    message = call(
        mean_kernel, shape((2 * pushed, narrow), BF), [vmem((2 * pushed, narrow), F32)],
        2 * halos * pushed * narrow, 4_000_000,
        incoming, near_counts, own_sum, push_act, push_count,
    )
    arrived = lax.all_to_all(
        message.reshape(doms * subs, 2 * cap, narrow), both, 0, 0, tiled=True
    ).reshape(2 * pushed, narrow)
    pairs = labels.shape[0]
    pair_loss, back = call(
        decode_kernel,
        (shape((1, pairs), F32), shape((pushed, narrow), BF)),
        [vmem((2 * pushed, narrow), F32), vmem((pushed, narrow), F32)],
        5_000_000_000, 5_000_000,
        arrived, w_self, w_nbr, w_pair, w_out.reshape(1, -1), jnp.transpose(pair_slots),
        labels.reshape(1, pairs),
    )
    returned = lax.all_to_all(
        back.reshape(doms * subs, cap, narrow), both, 0, 0, tiled=True
    ).reshape(pushed, narrow)
    embed_grad = call(
        owner_kernel, pltpu.HBM((firms, narrow), F32),
        [vmem((pushed, narrow), F32), vmem((firms, narrow), F32), pltpu.SemaphoreType.DMA((4,))],
        2 * pushed * firms * narrow, 1_000_000, returned, push_t,
        in_specs=[("vmem",)] * 2, out_specs=["hbm"],
    )
    return (pair_loss.reshape(pairs), embed_grad)


def solution(mesh):
    in_specs = (
        P("dom", "sub"), P(), P(), P("dom", None, None), P("dom", None), P("dom"), P(), P(),
        P("dom", None, None, None), P(("dom", "sub"), None), P(("dom", "sub")),
    )
    out_specs = (P(("dom", "sub")), P("dom", "sub"))
    return jax.shard_map(
        per_device, mesh=mesh, in_specs=in_specs, out_specs=out_specs, check_vma=False
    )
```

```python
import jax
import jax.numpy as jnp
from jax import lax
from jax.experimental import pallas as pl
from jax.experimental.pallas import tpu as pltpu
from jax.sharding import PartitionSpec as P

BF = jnp.bfloat16
F32 = jnp.float32
CORES = 2
YS = 8
DEAD = 4095
MIB = 1024 * 1024


def contract_first(a, b):
    return lax.dot_general(a, b, (((0,), (0,)), ((), ())), preferred_element_type=F32)


def call(kernel, out_shape, scratch, flops, nbytes, *args, in_specs=None, out_specs=None):
    where = {"hbm": pl.ANY, "vmem": pltpu.VMEM}
    specs = {}
    if in_specs is not None:
        args = [
            pltpu.with_memory_space_constraint(a, pltpu.HBM) if w[0] == "hbm" else a
            for a, w in zip(args, in_specs)
        ]
        specs["in_specs"] = [pl.BlockSpec(memory_space=where[w[-1]]) for w in in_specs]
    if out_specs is not None:
        specs["out_specs"] = [pl.BlockSpec(memory_space=where[w]) for w in out_specs]
        if len(out_specs) == 1:
            specs["out_specs"] = specs["out_specs"][0]
    return pl.pallas_call(
        kernel,
        out_shape=out_shape,
        scratch_shapes=scratch,
        **specs,
        compiler_params=pltpu.CompilerParams(vmem_limit_bytes=24 * MIB),
        cost_estimate=pl.CostEstimate(flops=flops, bytes_accessed=nbytes, transcendentals=0),
    )(*args)


def one_hot_rows(columns, width):
    number = lax.broadcasted_iota(jnp.int32, (columns.shape[0], width), 1)
    return [
        jnp.where(columns[:, j : j + 1] == number, 1.0, 0.0).astype(BF)
        for j in range(columns.shape[1])
    ]


def halo_kernel(act_ref, rows_ref, out_ref, pick_ref):
    slots, parts = rows_ref.shape
    rows = rows_ref[...]
    number = lax.broadcasted_iota(jnp.int32, (slots, act_ref.shape[0]), 1)
    zs = parts // YS // CORES
    order = [(y * zs + z) * CORES + c for z in range(zs) for y in range(YS) for c in range(CORES)]
    for at in range(0, parts, 2):
        pair = [
            jnp.where(rows[:, p : p + 1] == number, 1.0, 0.0) for p in order[at : at + 2]
        ]
        pick_ref[at * slots : (at + 2) * slots, :] = jnp.concatenate(pair, 0).astype(BF)
    out_ref[...] = jnp.dot(pick_ref[...], act_ref[...], preferred_element_type=F32).astype(BF)


def count_kernel(
    act_ref, push_ref, nbr_ref, cnt_ref, near_ref, own_ref, actp_ref, cntp_ref,
    pick_ref, mine_ref, where_ref,
):
    groups, parts = push_ref.shape
    firms = act_ref.shape[0]
    degree = nbr_ref.shape[0]
    pushed = groups * parts
    i32, i16 = jnp.int32, jnp.int16
    for j, rows in enumerate(one_hot_rows(push_ref[...].T, firms)):
        pick_ref[j * parts : (j + 1) * parts, :] = rows
    pick = pick_ref[...]
    count = cnt_ref[...]
    live = lax.broadcasted_iota(i32, (degree, firms), 0) < count
    slot = nbr_ref[...]
    cell = (near_ref.shape[1] // parts) * CORES
    zs = parts // YS // CORES
    past = slot - firms
    y, z = past // (cell * zs), past // cell % zs
    moved = firms + (z * YS + y) * cell + past % cell
    slot = jnp.where(live, jnp.where(past >= 0, moved, slot), DEAD)
    counts = jnp.broadcast_to(count, (degree, firms))
    stack = jnp.concatenate([slot >> 7, slot & 127, counts], 0).astype(F32).astype(BF)
    chosen = lax.dot_general(
        pick, stack, (((1,), (1,)), ((), ())), preferred_element_type=F32
    )
    for j in range(groups):
        block = chosen[j * parts : (j + 1) * parts, 2 * degree : 3 * degree]
        cntp_ref[j : j + 1, :] = block.T[0:1, :]
    actp_ref[...] = jnp.dot(pick, act_ref[...], preferred_element_type=F32).astype(BF)
    batch = 16
    span = batch * degree
    shape = (2 * degree, 2 * span)
    lane = lax.broadcasted_iota(i32, shape, 1)
    spread = jnp.where(
        lax.broadcasted_iota(i32, shape, 0) == (lane // span) * degree + lane % degree, 1.0, 0.0
    ).astype(BF)
    wide = jnp.dot(chosen[:, : 2 * degree].astype(BF), spread, preferred_element_type=F32)
    row = lax.broadcasted_iota(i32, (pushed, 2 * span), 0) % batch
    lane = (lax.broadcasted_iota(i32, (pushed, 2 * span), 1) % span) // degree
    wide = jnp.where(row == lane, wide, 0.0).astype(BF)
    shape = (pushed // batch, pushed)
    gather = jnp.where(
        lax.broadcasted_iota(i32, shape, 1) // batch == lax.broadcasted_iota(i32, shape, 0), 1.0, 0.0
    ).astype(BF)
    where_ref[...] = jnp.dot(gather, wide, preferred_element_type=F32)
    own_row = (
        lax.broadcasted_iota(i32, (batch, span), 1) // degree
        == lax.broadcasted_iota(i32, (batch, span), 0)
    )
    low_number = lax.broadcasted_iota(i32, (128, span), 0).astype(i16)
    one = jnp.ones((batch, span), BF)
    zero = jnp.zeros((batch, span), BF)
    mine_blocks = firms // 128
    near_blocks = near_ref.shape[1] // 128

    def fill(g, carry):
        line = where_ref[pl.ds(g, 1), :]
        high = jnp.where(own_row, jnp.broadcast_to(line[:, :span], (batch, span)), -1.0)
        high = high.astype(i32).astype(i16)
        lhs = jnp.concatenate(
            [jnp.where(high == i16(h), one, zero) for h in range(mine_blocks + near_blocks)], 0
        )
        low = jnp.broadcast_to(line[:, span:], (128, span)).astype(i32).astype(i16)
        rhs = jnp.where(low == low_number, jnp.ones((128, span), BF), jnp.zeros((128, span), BF))
        counts = lax.dot_general(
            lhs, rhs, (((1,), (1,)), ((), ())), preferred_element_type=F32
        ).astype(BF)
        rows = pl.ds(pl.multiple_of(g * batch, batch), batch)
        for h in range(mine_blocks):
            mine_ref[rows, h * 128 : (h + 1) * 128] = counts[h * batch : (h + 1) * batch]
        for h in range(near_blocks):
            at = (mine_blocks + h) * batch
            near_ref[rows, h * 128 : (h + 1) * 128] = counts[at : at + batch]
        return carry

    lax.fori_loop(0, pushed // batch, fill, 0, unroll=4)
    own_ref[...] = jnp.dot(mine_ref[...], act_ref[...], preferred_element_type=F32)


def mean_kernel(halo_ref, near_ref, own_ref, actp_ref, cntp_ref, out_ref, tmp_ref):
    groups, parts = cntp_ref.shape
    divisor = cntp_ref[...].T
    summed = own_ref[...] + jnp.dot(near_ref[...], halo_ref[...], preferred_element_type=F32)

    def place(b, rows, kind):
        tmp_ref[pl.ds((b // 2) * parts * 4 + kind * 2 + b % 2, parts, stride=4), :] = rows

    for b in range(groups):
        rows = slice(b * parts, (b + 1) * parts)
        place(b, actp_ref[rows, :].astype(F32), 0)
        mean = summed[rows] / divisor[:, b : b + 1]
        place(b, mean.astype(BF).astype(F32), 1)
    out_ref[...] = tmp_ref[...].astype(BF)


def decode_kernel(
    recv_ref, self_ref, near_ref, pair_ref, wout_ref, slots_ref, label_ref,
    loss_ref, out_ref, tmp_ref, back_ref,
):
    parts = recv_ref.shape[0] // 16
    pairs = slots_ref.shape[1]
    width = self_ref.shape[0]
    tmp_ref[...] = recv_ref[...].astype(F32)

    def rows_of(kind):
        halves = [
            jnp.concatenate(
                [
                    tmp_ref[pl.ds(s * parts * 4 + kind * 2 + c, parts, stride=4), :]
                    for s in range(4)
                ],
                1,
            )
            for c in range(2)
        ]
        return jnp.concatenate(halves, 0).astype(BF)

    embed = (
        jnp.dot(rows_of(0), self_ref[...], preferred_element_type=F32)
        + jnp.dot(rows_of(1), near_ref[...], preferred_element_type=F32)
    ).astype(BF)
    place = lax.broadcasted_iota(jnp.int32, (2 * parts, pairs), 0)
    slot = jnp.where(place < parts, 2 * place, 2 * (place - parts) + 1)
    left_pick = jnp.where(slot == slots_ref[0:1, :], 1.0, 0.0).astype(BF)
    right_pick = jnp.where(slot == slots_ref[1:2, :], 1.0, 0.0).astype(BF)
    picks = jnp.concatenate([left_pick, right_pick], 1)
    ends = contract_first(picks, embed)
    left, right = ends[:pairs], ends[pairs:]
    product = (left * right).astype(BF)
    pre_act = (
        jnp.dot(left.astype(BF), pair_ref[0:width, :], preferred_element_type=F32)
        + jnp.dot(right.astype(BF), pair_ref[width : 2 * width, :], preferred_element_type=F32)
        + jnp.dot(product, pair_ref[2 * width : 3 * width, :], preferred_element_type=F32)
    )
    gate = jax.nn.sigmoid(pre_act)
    active = pre_act * gate
    wout = wout_ref[...]
    logit = jnp.sum(active * wout, axis=1, keepdims=True)
    target = jnp.broadcast_to(label_ref[...].astype(F32), (pairs, pairs)).T[:, 0:1]
    loss = jnp.maximum(logit, 0.0) + jnp.log1p(jnp.exp(-jnp.abs(logit))) - target * logit
    loss_ref[...] = jnp.broadcast_to(loss, (pairs, pairs)).T[0:1, :]
    outer = jax.nn.sigmoid(logit) - target
    pre_grad = (wout * (gate + active * (1.0 - gate))).astype(BF)
    feat = [
        lax.dot_general(
            pre_grad, pair_ref[i * width : (i + 1) * width, :], (((1,), (1,)), ((), ())),
            preferred_element_type=F32,
        )
        for i in (2, 0, 1)
    ]
    third = outer * feat[0]
    left_grad = (outer * feat[1] + third * right).astype(BF)
    right_grad = (outer * feat[2] + third * left).astype(BF)
    back = jnp.dot(
        picks, jnp.concatenate([left_grad, right_grad], 0), preferred_element_type=F32
    )
    for s in range(4):
        for c in range(2):
            back_ref[pl.ds(s * parts * 2 + c, parts, stride=2), :] = back[
                c * parts : (c + 1) * parts, s * 128 : (s + 1) * 128
            ]
    out_ref[...] = back_ref[...].astype(BF)


def owner_kernel(recv_ref, push_ref, out_ref, tmp_ref, sum_ref, sems):
    groups, parts = push_ref.shape
    tmp_ref[...] = recv_ref[...].astype(F32)
    grads = jnp.concatenate(
        [tmp_ref[pl.ds((b // 2) * parts * 2 + b % 2, parts, stride=2), :]
            for b in range(groups)], 0
    ).astype(BF)
    parcels = sems.shape[0]
    step = sum_ref.shape[0] // parcels
    firm = lax.broadcasted_iota(jnp.int32, (step, parts), 0)
    copies = []
    for p in range(parcels):
        pick = jnp.concatenate(
            [
                jnp.where(firm + p * step == push_ref[b : b + 1, :], 1.0, 0.0).astype(BF)
                for b in range(groups)
            ],
            1,
        )
        rows = pl.ds(p * step, step)
        sum_ref[rows, :] = jnp.dot(pick, grads, preferred_element_type=F32)
        copies.append(pltpu.make_async_copy(sum_ref.at[rows, :], out_ref.at[rows, :], sems.at[p]))
        copies[-1].start()
    for copy in copies:
        copy.wait()


def per_device(
    firm_act, w_self, w_nbr, halo_rows, nbr_index, nbr_count, w_pair, w_out, push_rows,
    pair_slots, labels,
):
    firms, narrow = firm_act.shape
    doms, subs, cap = push_rows.shape[1:]
    slots = halo_rows.shape[2]
    both = ("x", "y", "z", "c")
    shape = jax.ShapeDtypeStruct
    vmem = pltpu.VMEM
    halo_t = jnp.transpose(halo_rows[0])
    push_t = jnp.transpose(push_rows[0], (1, 2, 0)).reshape(subs * cap, doms)
    pushed = doms * subs * cap
    halos = doms * slots

    fetch = ("hbm", "vmem")
    outgoing = call(
        halo_kernel, shape((halos, narrow), BF), [vmem((halos, firms), BF)],
        2 * halos * firms * narrow, 600_000, firm_act, halo_t, in_specs=[fetch, fetch],
    )
    incoming = lax.all_to_all(
        outgoing.reshape(doms, slots, narrow), ("z", "y", "c"), 0, 0, tiled=True
    ).reshape(halos, narrow)
    near_counts, own_sum, push_act, push_count = call(
        count_kernel,
        (
            shape((pushed, halos), BF), shape((pushed, narrow), F32), shape((pushed, narrow), BF),
            shape((subs * cap, doms), F32),
        ),
        [vmem((pushed, firms), BF), vmem((pushed, firms), BF), vmem((pushed // 16, 512), F32)],
        10_000_000_000, 4_000_000,
        firm_act, push_t, jnp.transpose(nbr_index), nbr_count.reshape(1, firms),
        in_specs=[fetch] * 4,
    )
    message = call(
        mean_kernel, shape((2 * pushed, narrow), BF), [vmem((2 * pushed, narrow), F32)],
        2 * halos * pushed * narrow, 4_000_000,
        incoming, near_counts, own_sum, push_act, push_count,
    )
    arrived = lax.all_to_all(
        message.reshape(doms * subs, 2 * cap, narrow), both, 0, 0, tiled=True
    ).reshape(2 * pushed, narrow)
    pairs = labels.shape[0]
    pair_loss, back = call(
        decode_kernel,
        (shape((1, pairs), F32), shape((pushed, narrow), BF)),
        [vmem((2 * pushed, narrow), F32), vmem((pushed, narrow), F32)],
        5_000_000_000, 5_000_000,
        arrived, w_self, w_nbr, w_pair, w_out.reshape(1, -1), jnp.transpose(pair_slots),
        labels.reshape(1, pairs),
    )
    returned = lax.all_to_all(
        back.reshape(doms * subs, cap, narrow), both, 0, 0, tiled=True
    ).reshape(pushed, narrow)
    embed_grad = call(
        owner_kernel, pltpu.HBM((firms, narrow), F32),
        [vmem((pushed, narrow), F32), vmem((firms, narrow), F32), pltpu.SemaphoreType.DMA((4,))],
        2 * pushed * firms * narrow, 1_000_000, returned, push_t,
        in_specs=[("vmem",)] * 2, out_specs=["hbm"],
    )
    return (pair_loss.reshape(pairs), embed_grad)


def solution(mesh):
    subs = mesh.shape["sub"]
    zs = mesh.shape["dom"] // YS // CORES
    cut = jax.sharding.Mesh(mesh.devices.reshape(YS, zs, CORES, subs), ("y", "z", "c", "x"))
    dom, every = ("y", "z", "c"), ("y", "z", "c", "x")
    in_specs = (
        P(dom, "x"), P(), P(), P(dom, None, None), P(dom, None), P(dom), P(), P(),
        P(dom, None, None, None), P(every, None), P(every),
    )
    out_specs = (P(every), P(dom, "x"))
    return jax.shard_map(
        per_device, mesh=cut, in_specs=in_specs, out_specs=out_specs, check_vma=False
    )
```

```python
import jax
import jax.numpy as jnp
from jax import lax
from jax.experimental import pallas as pl
from jax.experimental.pallas import tpu as pltpu
from jax.sharding import PartitionSpec as P

BF = jnp.bfloat16
F32 = jnp.float32
DEAD = 4095
MIB = 1024 * 1024


def contract_first(a, b):
    return lax.dot_general(a, b, (((0,), (0,)), ((), ())), preferred_element_type=F32)


def call(kernel, out_shape, scratch, flops, nbytes, *args, in_specs=None, out_specs=None):
    where = {"hbm": pl.ANY, "vmem": pltpu.VMEM}
    specs = {}
    if in_specs is not None:
        args = [
            pltpu.with_memory_space_constraint(a, pltpu.HBM) if w[0] == "hbm" else a
            for a, w in zip(args, in_specs)
        ]
        specs["in_specs"] = [pl.BlockSpec(memory_space=where[w[-1]]) for w in in_specs]
    if out_specs is not None:
        specs["out_specs"] = [pl.BlockSpec(memory_space=where[w]) for w in out_specs]
        if len(out_specs) == 1:
            specs["out_specs"] = specs["out_specs"][0]
    return pl.pallas_call(
        kernel,
        out_shape=out_shape,
        scratch_shapes=scratch,
        **specs,
        compiler_params=pltpu.CompilerParams(vmem_limit_bytes=24 * MIB),
        cost_estimate=pl.CostEstimate(flops=flops, bytes_accessed=nbytes, transcendentals=0),
    )(*args)


def one_hot_rows(columns, width):
    number = lax.broadcasted_iota(jnp.int32, (columns.shape[0], width), 1)
    return [
        jnp.where(columns[:, j : j + 1] == number, 1.0, 0.0).astype(BF)
        for j in range(columns.shape[1])
    ]


def halo_kernel(act_ref, rows_ref, out_ref, pick_ref):
    slots, parts = rows_ref.shape
    rows = rows_ref[...]
    number = lax.broadcasted_iota(jnp.int32, (slots, act_ref.shape[0]), 1)
    for at in range(0, parts, 2):
        pair = [jnp.where(rows[:, p : p + 1] == number, 1.0, 0.0) for p in (at, at + 1)]
        pick_ref[at * slots : (at + 2) * slots, :] = jnp.concatenate(pair, 0).astype(BF)
    out_ref[...] = jnp.dot(pick_ref[...], act_ref[...], preferred_element_type=F32).astype(BF)


def count_kernel(
    act_ref, push_ref, nbr_ref, cnt_ref, near_ref, own_ref, actp_ref, cntp_ref,
    pick_ref, mine_ref, where_ref,
):
    groups, parts = push_ref.shape
    firms = act_ref.shape[0]
    degree = nbr_ref.shape[0]
    pushed = groups * parts
    i32, i16 = jnp.int32, jnp.int16
    for j, rows in enumerate(one_hot_rows(push_ref[...].T, firms)):
        pick_ref[j * parts : (j + 1) * parts, :] = rows
    pick = pick_ref[...]
    count = cnt_ref[...]
    live = lax.broadcasted_iota(i32, (degree, firms), 0) < count
    slot = jnp.where(live, nbr_ref[...], DEAD)
    counts = jnp.broadcast_to(count, (degree, firms))
    stack = jnp.concatenate([slot >> 7, slot & 127, counts], 0).astype(F32).astype(BF)
    chosen = lax.dot_general(
        pick, stack, (((1,), (1,)), ((), ())), preferred_element_type=F32
    )
    for j in range(groups):
        block = chosen[j * parts : (j + 1) * parts, 2 * degree : 3 * degree]
        cntp_ref[j : j + 1, :] = block.T[0:1, :]
    actp_ref[...] = jnp.dot(pick, act_ref[...], preferred_element_type=F32).astype(BF)
    batch = 16
    span = batch * degree
    shape = (2 * degree, 2 * span)
    lane = lax.broadcasted_iota(i32, shape, 1)
    spread = jnp.where(
        lax.broadcasted_iota(i32, shape, 0) == (lane // span) * degree + lane % degree, 1.0, 0.0
    ).astype(BF)
    wide = jnp.dot(chosen[:, : 2 * degree].astype(BF), spread, preferred_element_type=F32)
    row = lax.broadcasted_iota(i32, (pushed, 2 * span), 0) % batch
    lane = (lax.broadcasted_iota(i32, (pushed, 2 * span), 1) % span) // degree
    wide = jnp.where(row == lane, wide, 0.0).astype(BF)
    shape = (pushed // batch, pushed)
    gather = jnp.where(
        lax.broadcasted_iota(i32, shape, 1) // batch == lax.broadcasted_iota(i32, shape, 0), 1.0, 0.0
    ).astype(BF)
    where_ref[...] = jnp.dot(gather, wide, preferred_element_type=F32)
    own_row = (
        lax.broadcasted_iota(i32, (batch, span), 1) // degree
        == lax.broadcasted_iota(i32, (batch, span), 0)
    )
    low_number = lax.broadcasted_iota(i32, (128, span), 0).astype(i16)
    one = jnp.ones((batch, span), BF)
    zero = jnp.zeros((batch, span), BF)
    mine_blocks = firms // 128
    near_blocks = near_ref.shape[1] // 128

    def fill(g, carry):
        line = where_ref[pl.ds(g, 1), :]
        high = jnp.where(own_row, jnp.broadcast_to(line[:, :span], (batch, span)), -1.0)
        high = high.astype(i32).astype(i16)
        lhs = jnp.concatenate(
            [jnp.where(high == i16(h), one, zero) for h in range(mine_blocks + near_blocks)], 0
        )
        low = jnp.broadcast_to(line[:, span:], (128, span)).astype(i32).astype(i16)
        rhs = jnp.where(low == low_number, jnp.ones((128, span), BF), jnp.zeros((128, span), BF))
        counts = lax.dot_general(
            lhs, rhs, (((1,), (1,)), ((), ())), preferred_element_type=F32
        ).astype(BF)
        rows = pl.ds(pl.multiple_of(g * batch, batch), batch)
        for h in range(mine_blocks):
            mine_ref[rows, h * 128 : (h + 1) * 128] = counts[h * batch : (h + 1) * batch]
        for h in range(near_blocks):
            at = (mine_blocks + h) * batch
            near_ref[rows, h * 128 : (h + 1) * 128] = counts[at : at + batch]
        return carry

    lax.fori_loop(0, pushed // batch, fill, 0, unroll=4)
    own_ref[...] = jnp.dot(mine_ref[...], act_ref[...], preferred_element_type=F32)


def mean_kernel(halo_ref, near_ref, own_ref, actp_ref, cntp_ref, out_ref, tmp_ref):
    groups, parts = cntp_ref.shape
    divisor = cntp_ref[...].T
    summed = own_ref[...] + jnp.dot(near_ref[...], halo_ref[...], preferred_element_type=F32)

    def place(b, rows, kind):
        tmp_ref[pl.ds((b // 2) * parts * 4 + kind * 2 + b % 2, parts, stride=4), :] = rows

    for b in range(groups):
        rows = slice(b * parts, (b + 1) * parts)
        place(b, actp_ref[rows, :].astype(F32), 0)
        mean = summed[rows] / divisor[:, b : b + 1]
        place(b, mean.astype(BF).astype(F32), 1)
    out_ref[...] = tmp_ref[...].astype(BF)


def decode_kernel(
    recv_ref, self_ref, near_ref, pair_ref, wout_ref, slots_ref, label_ref,
    loss_ref, out_ref, tmp_ref, back_ref,
):
    parts = recv_ref.shape[0] // 16
    pairs = slots_ref.shape[1]
    width = self_ref.shape[0]
    tmp_ref[...] = recv_ref[...].astype(F32)

    def rows_of(kind):
        halves = [
            jnp.concatenate(
                [
                    tmp_ref[pl.ds(s * parts * 4 + kind * 2 + c, parts, stride=4), :]
                    for s in range(4)
                ],
                1,
            )
            for c in range(2)
        ]
        return jnp.concatenate(halves, 0).astype(BF)

    embed = (
        jnp.dot(rows_of(0), self_ref[...], preferred_element_type=F32)
        + jnp.dot(rows_of(1), near_ref[...], preferred_element_type=F32)
    ).astype(BF)
    place = lax.broadcasted_iota(jnp.int32, (2 * parts, pairs), 0)
    slot = jnp.where(place < parts, 2 * place, 2 * (place - parts) + 1)
    left_pick = jnp.where(slot == slots_ref[0:1, :], 1.0, 0.0).astype(BF)
    right_pick = jnp.where(slot == slots_ref[1:2, :], 1.0, 0.0).astype(BF)
    picks = jnp.concatenate([left_pick, right_pick], 1)
    ends = contract_first(picks, embed)
    left, right = ends[:pairs], ends[pairs:]
    product = (left * right).astype(BF)
    pre_act = (
        jnp.dot(left.astype(BF), pair_ref[0:width, :], preferred_element_type=F32)
        + jnp.dot(right.astype(BF), pair_ref[width : 2 * width, :], preferred_element_type=F32)
        + jnp.dot(product, pair_ref[2 * width : 3 * width, :], preferred_element_type=F32)
    )
    gate = jax.nn.sigmoid(pre_act)
    active = pre_act * gate
    wout = wout_ref[...]
    logit = jnp.sum(active * wout, axis=1, keepdims=True)
    target = jnp.broadcast_to(label_ref[...].astype(F32), (pairs, pairs)).T[:, 0:1]
    loss = jnp.maximum(logit, 0.0) + jnp.log1p(jnp.exp(-jnp.abs(logit))) - target * logit
    loss_ref[...] = jnp.broadcast_to(loss, (pairs, pairs)).T[0:1, :]
    outer = jax.nn.sigmoid(logit) - target
    pre_grad = (wout * (gate + active * (1.0 - gate))).astype(BF)
    feat = [
        lax.dot_general(
            pre_grad, pair_ref[i * width : (i + 1) * width, :], (((1,), (1,)), ((), ())),
            preferred_element_type=F32,
        )
        for i in (2, 0, 1)
    ]
    third = outer * feat[0]
    left_grad = (outer * feat[1] + third * right).astype(BF)
    right_grad = (outer * feat[2] + third * left).astype(BF)
    back = jnp.dot(
        picks, jnp.concatenate([left_grad, right_grad], 0), preferred_element_type=F32
    )
    for s in range(4):
        for c in range(2):
            back_ref[pl.ds(s * parts * 2 + c, parts, stride=2), :] = back[
                c * parts : (c + 1) * parts, s * 128 : (s + 1) * 128
            ]
    out_ref[...] = back_ref[...].astype(BF)


def owner_kernel(recv_ref, push_ref, out_ref, tmp_ref, sum_ref, sems):
    groups, parts = push_ref.shape
    tmp_ref[...] = recv_ref[...].astype(F32)
    grads = jnp.concatenate(
        [tmp_ref[pl.ds((b // 2) * parts * 2 + b % 2, parts, stride=2), :]
            for b in range(groups)], 0
    ).astype(BF)
    parcels = sems.shape[0]
    step = sum_ref.shape[0] // parcels
    firm = lax.broadcasted_iota(jnp.int32, (step, parts), 0)
    copies = []
    for p in range(parcels):
        pick = jnp.concatenate(
            [
                jnp.where(firm + p * step == push_ref[b : b + 1, :], 1.0, 0.0).astype(BF)
                for b in range(groups)
            ],
            1,
        )
        rows = pl.ds(p * step, step)
        sum_ref[rows, :] = jnp.dot(pick, grads, preferred_element_type=F32)
        copies.append(pltpu.make_async_copy(sum_ref.at[rows, :], out_ref.at[rows, :], sems.at[p]))
        copies[-1].start()
    for copy in copies:
        copy.wait()


def per_device(
    firm_act, w_self, w_nbr, halo_rows, nbr_index, nbr_count, w_pair, w_out, push_rows,
    pair_slots, labels,
):
    firms, narrow = firm_act.shape
    doms, subs, cap = push_rows.shape[1:]
    slots = halo_rows.shape[2]
    both = ("sub", "dom")
    shape = jax.ShapeDtypeStruct
    vmem = pltpu.VMEM
    halo_t = jnp.transpose(halo_rows[0])
    push_t = jnp.transpose(push_rows[0], (1, 2, 0)).reshape(subs * cap, doms)
    pushed = doms * subs * cap
    halos = doms * slots

    fetch = ("hbm", "vmem")
    outgoing = call(
        halo_kernel, shape((halos, narrow), BF), [vmem((halos, firms), BF)],
        2 * halos * firms * narrow, 600_000, firm_act, halo_t, in_specs=[fetch, fetch],
    )
    incoming = lax.all_to_all(
        outgoing.reshape(doms, slots, narrow), "dom", 0, 0, tiled=True
    ).reshape(halos, narrow)
    near_counts, own_sum, push_act, push_count = call(
        count_kernel,
        (
            shape((pushed, halos), BF), shape((pushed, narrow), F32), shape((pushed, narrow), BF),
            shape((subs * cap, doms), F32),
        ),
        [vmem((pushed, firms), BF), vmem((pushed, firms), BF), vmem((pushed // 16, 512), F32)],
        10_000_000_000, 4_000_000,
        firm_act, push_t, jnp.transpose(nbr_index), nbr_count.reshape(1, firms),
        in_specs=[fetch] * 4,
    )
    message = call(
        mean_kernel, shape((2 * pushed, narrow), BF), [vmem((2 * pushed, narrow), F32)],
        2 * halos * pushed * narrow, 4_000_000,
        incoming, near_counts, own_sum, push_act, push_count,
    )
    arrived = lax.all_to_all(
        message.reshape(doms * subs, 2 * cap, narrow), both, 0, 0, tiled=True
    ).reshape(2 * pushed, narrow)
    pairs = labels.shape[0]
    pair_loss, back = call(
        decode_kernel,
        (shape((1, pairs), F32), shape((pushed, narrow), BF)),
        [vmem((2 * pushed, narrow), F32), vmem((pushed, narrow), F32)],
        5_000_000_000, 5_000_000,
        arrived, w_self, w_nbr, w_pair, w_out.reshape(1, -1), jnp.transpose(pair_slots),
        labels.reshape(1, pairs),
    )
    returned = lax.all_to_all(
        back.reshape(doms * subs, cap, narrow), both, 0, 0, tiled=True
    ).reshape(pushed, narrow)
    embed_grad = call(
        owner_kernel, pltpu.HBM((firms, narrow), F32),
        [vmem((pushed, narrow), F32), vmem((firms, narrow), F32), pltpu.SemaphoreType.DMA((4,))],
        2 * pushed * firms * narrow, 1_000_000, returned, push_t,
        in_specs=[("vmem",)] * 2, out_specs=["hbm"],
    )
    return (pair_loss.reshape(pairs), embed_grad)


def solution(mesh):
    in_specs = (
        P("dom", "sub"), P(), P(), P("dom", None, None), P("dom", None), P("dom"), P(), P(),
        P("dom", None, None, None), P(("dom", "sub"), None), P(("dom", "sub")),
    )
    out_specs = (P(("dom", "sub")), P("dom", "sub"))
    return jax.shard_map(
        per_device, mesh=mesh, in_specs=in_specs, out_specs=out_specs, check_vma=False
    )
```
